512 devices in a mesh: ctx: 32 (over y, x), dp: 16 (over z, core).
Axes of the slice: x: 4, y: 8, z: 8, core: 2. Of those that a mesh axis runs over, the one named last changes fastest.
Arguments:
- query_in: bfloat16 [16384, 8192], P('ctx', 'dp'), may hold values from -6 to 6
- key_in: bfloat16 [16384, 8192], P('ctx', 'dp'), may hold values from -6 to 6
- value_in: bfloat16 [16384, 8192], P('ctx', 'dp'), may hold values from -280 to 280
- log_decay: float32 [64, 16384], P('dp', 'ctx'), may hold values from -0.8 to 0
- norm_gain: float32 [8192], P('dp'), may hold values from 0.25 to 1.75
- grad_out: bfloat16 [16384, 8192], P('ctx', 'dp'), may hold values from -6 to 6
Outputs:
- attended: bfloat16 [16384, 8192], P('ctx', 'dp')
- grad_query: bfloat16 [16384, 8192], P('ctx', 'dp')
- grad_key: bfloat16 [16384, 8192], P('ctx', 'dp')
- grad_value: bfloat16 [16384, 8192], P('ctx', 'dp')
- grad_gain: float32 [8192], P('dp')
The draws below stay inside these ranges and needn't reach their ends.
All inputs are finite; a program needn't handle non-finite values.
Results may differ from the reference program's by a relative error of at most 0.011.
Values sent between devices are 32-bit elements; how exact they have to be, the bound alone decides.
A program may use at most 64 MiB of HBM per device.

```python
import math
import jax
import jax.numpy as jnp
from jax import lax

HEADS = 64
HEAD = 128
TOK_DEV = 512
BLOCK = 512
TOKEN_POSITIONS = 16384
FEATURES = 8192


def draw_log_decay(key, part):
    key = jax.random.fold_in(key, 11)
    segment_parts = jax.random.split(key, 8)
    fast_share = 0.5
    fast_heads = jax.random.uniform(segment_parts[0], (HEADS, 1)) < fast_share
    slow_rate = jax.random.uniform(segment_parts[1], (HEADS, 1), minval=0.15, maxval=0.6) / TOKEN_POSITIONS
    fast_rate = jnp.exp(jax.random.uniform(segment_parts[2], (HEADS, 1), minval=math.log(1.0 / 50.0), maxval=math.log(1.0 / 30.0)))
    baseline_rate = jnp.where(fast_heads, fast_rate, slow_rate)
    jaggedness = jax.random.uniform(segment_parts[3], (HEADS, TOKEN_POSITIONS), minval=0.5, maxval=1.5)
    device_factor = jnp.exp(jax.random.uniform(segment_parts[4], (TOKEN_POSITIONS // TOK_DEV,), minval=math.log(0.7), maxval=math.log(1.4)))
    dispersal_factor = jnp.repeat(device_factor, TOK_DEV)[None, :]
    midpoint_length = TOKEN_POSITIONS // 2
    leading_spike = jax.random.randint(segment_parts[5], (), 0, midpoint_length)
    trailing_spike = jax.random.randint(segment_parts[6], (), midpoint_length, TOKEN_POSITIONS)
    loss_values = jax.random.uniform(segment_parts[7], (HEADS, 2), minval=0.2, maxval=0.5)
    token_places = jnp.arange(TOKEN_POSITIONS)[None, :]
    spike_loss = jnp.where(token_places == leading_spike, jnp.log(1.0 - loss_values[:, 0:1]), 0.0)
    spike_loss = spike_loss + jnp.where(token_places == trailing_spike, jnp.log(1.0 - loss_values[:, 1:2]), 0.0)
    return (-baseline_rate * jaggedness * dispersal_factor + spike_loss).astype(jnp.float32)


def draw_value_in(key, part):
    key = jax.random.fold_in(key, 23)
    segment_parts = jax.random.split(key, 4)
    head_index = jnp.arange(FEATURES) // HEAD
    column_scale = jnp.exp(jax.random.uniform(segment_parts[0], (FEATURES,), minval=0.0, maxval=math.log(10.0)))
    column_scale = column_scale * jnp.exp(math.log(3.0) * head_index / max(HEADS - 1, 1)) / 4.0
    entries = jnp.clip(jax.random.normal(segment_parts[3], (TOKEN_POSITIONS, FEATURES)), -4.0, 4.0)
    return (entries * column_scale[None, :]).astype(jnp.bfloat16)


def shard_levels(stream_key, shape, pieces, smallest, high):
    def one(position, blocks):
        heights = jax.random.uniform(jax.random.fold_in(jax.random.fold_in(stream_key, 6), position), (blocks,), jnp.float32, smallest / len(pieces), high / len(pieces))
        return jnp.repeat(jnp.exp(heights), shape[position] // blocks).reshape((-1,) + (1,) * (len(shape) - position - 1))

    level = one(*pieces[0])
    for cut in pieces[1:]:
        level = level * one(*cut)
    return level


def noise(stream_key, extent, spread, limit, pieces=(), held_as=jnp.bfloat16):
    values = spread * jax.random.normal(stream_key, extent, jnp.float32)
    if pieces:
        values = values * shard_levels(stream_key, extent, pieces, -0.22, 0.18)
    return jnp.clip(values, -limit, limit).astype(held_as)


def setup_inputs(seed: int = 0) -> dict:
    key_list = jax.random.split(jax.random.key(seed), 7)
    return {
        "query_in": noise(key_list[0], (TOKEN_POSITIONS, FEATURES), 1.0, 6.0, ((0, 32), (1, 16))),
        "key_in": noise(key_list[1], (TOKEN_POSITIONS, FEATURES), 1.0, 6.0, ((0, 32), (1, 16))),
        "value_in": draw_value_in(jax.random.fold_in(key_list[6], 71), 0),
        "log_decay": draw_log_decay(jax.random.fold_in(key_list[6], 71), 0),
        "norm_gain": jnp.clip(1.0 + 0.15 * jax.random.normal(key_list[4], (FEATURES,), jnp.float32), 0.25, 1.75),
        "grad_out": noise(key_list[5], (TOKEN_POSITIONS, FEATURES), 1.0, 6.0, ((0, 32), (1, 16))),
    }


def decay_table(within):
    within_heads = within.T
    causal_mask = jnp.arange(BLOCK)[:, None] >= jnp.arange(BLOCK)[None, :]
    decay_gap = within_heads[:, :, None] - within_heads[:, None, :]
    return jnp.where(causal_mask, jnp.exp(jnp.where(causal_mask, decay_gap, 0.0)), 0.0)

def forward_block(carry_state, inputs):
    query_rows, key_rows, value_rows, within = inputs
    block_total = within[-1]
    decay_weights = decay_table(within)
    scores = jnp.einsum('thd,shd->hts', query_rows.astype(jnp.float32), key_rows.astype(jnp.float32))
    weighted = (scores * decay_weights).astype(jnp.bfloat16)
    local_mix = jnp.einsum('hts,shj->thj', weighted.astype(jnp.float32), value_rows.astype(jnp.float32))
    query_scaled = query_rows.astype(jnp.float32) * jnp.exp(within)[:, :, None]
    carried = jnp.einsum('thi,hij->thj', query_scaled, carry_state, precision=lax.Precision.HIGHEST)
    key_weighted = (key_rows.astype(jnp.float32) * jnp.exp(block_total[None, :] - within)[:, :, None]).astype(jnp.bfloat16)
    block_state = jnp.einsum('shi,shj->hij', key_weighted.astype(jnp.float32), value_rows.astype(jnp.float32))
    next_state = jnp.exp(block_total)[:, None, None] * carry_state + block_state
    return (next_state, (carried + local_mix, carry_state))

def backward_block(back_state, inputs):
    query_rows, key_rows, value_rows, within, start_state, grad_rows = inputs
    block_total = within[-1]
    decay_weights = decay_table(within)
    query_float = query_rows.astype(jnp.float32)
    key_float = key_rows.astype(jnp.float32)
    value_float = value_rows.astype(jnp.float32)
    grad_float = grad_rows.astype(jnp.float32)
    scores = jnp.einsum('thd,shd->hts', query_float, key_float)
    weighted = (scores * decay_weights).astype(jnp.bfloat16)
    grad_scores = jnp.einsum('thj,shj->hts', grad_float, value_float)
    grad_weighted = (grad_scores * decay_weights).astype(jnp.bfloat16).astype(jnp.float32)
    local_query = jnp.einsum('hts,shi->thi', grad_weighted, key_float)
    local_key = jnp.einsum('hts,thi->shi', grad_weighted, query_float)
    local_value = jnp.einsum('hts,thj->shj', weighted.astype(jnp.float32), grad_float)
    query_carried = jnp.exp(within)[:, :, None] * jnp.einsum('thj,hij->thi', grad_float, start_state, precision=lax.Precision.HIGHEST)
    tail_decay = jnp.exp(block_total[None, :] - within)[:, :, None]
    key_carried = tail_decay * jnp.einsum('shj,hij->shi', value_float, back_state, precision=lax.Precision.HIGHEST)
    value_carried = tail_decay * jnp.einsum('shi,hij->shj', key_float, back_state, precision=lax.Precision.HIGHEST)
    query_weighted = (query_float * jnp.exp(within)[:, :, None]).astype(jnp.bfloat16)
    block_back = jnp.einsum('uhi,uhj->hij', query_weighted.astype(jnp.float32), grad_float)
    next_back = jnp.exp(block_total)[:, None, None] * back_state + block_back
    outputs = ((query_carried + local_query).astype(jnp.bfloat16), (key_carried + local_key).astype(jnp.bfloat16), (value_carried + local_value).astype(jnp.bfloat16))
    return (next_back, outputs)

def reference(query_in, key_in, value_in, log_decay, norm_gain, grad_out):
    block_count = TOKEN_POSITIONS // BLOCK
    shaped = (block_count, BLOCK, HEADS, HEAD)
    query_rows = query_in.reshape(shaped)
    key_rows = key_in.reshape(shaped)
    value_rows = value_in.reshape(shaped)
    within = jnp.transpose(jnp.cumsum(log_decay.reshape(HEADS, block_count, BLOCK), axis=2), (1, 2, 0))
    zero_state = jnp.zeros((HEADS, HEAD, HEAD), jnp.float32)
    final_state, (raw_blocks, start_states) = lax.scan(forward_block, zero_state, (query_rows, key_rows, value_rows, within))
    raw_out = raw_blocks.reshape(TOKEN_POSITIONS, FEATURES)
    grad_float = grad_out.astype(jnp.float32)
    scaled_grad = grad_float * norm_gain
    square_sum = lax.optimization_barrier(jnp.sum(raw_out * raw_out, axis=1))
    cross_sum = lax.optimization_barrier(jnp.sum(scaled_grad * raw_out, axis=1))
    inv_rms = lax.rsqrt(square_sum / FEATURES + 1e-06)
    normed = raw_out * inv_rms[:, None]
    attended = (normed * norm_gain).astype(jnp.bfloat16)
    cubed = inv_rms * inv_rms * inv_rms
    grad_raw = (inv_rms[:, None] * scaled_grad - raw_out * cubed[:, None] * cross_sum[:, None] / FEATURES).astype(jnp.bfloat16)
    grad_gain = lax.optimization_barrier(jnp.sum(grad_float * normed, axis=0)) / math.sqrt(TOKEN_POSITIONS)
    grad_rows = grad_raw.reshape(shaped)
    final_back, (query_blocks, key_blocks, value_blocks) = lax.scan(backward_block, zero_state, (query_rows, key_rows, value_rows, within, start_states, grad_rows), reverse=True)
    grad_query = query_blocks.reshape(TOKEN_POSITIONS, FEATURES)
    grad_key = key_blocks.reshape(TOKEN_POSITIONS, FEATURES)
    grad_value = value_blocks.reshape(TOKEN_POSITIONS, FEATURES)
    return (attended, grad_query, grad_key, grad_value, grad_gain)
```

```python
import functools
import math

import jax
import jax.numpy as jnp
from jax import lax
from jax.experimental import pallas as pl
from jax.experimental.pallas import tpu as pltpu
from jax.sharding import PartitionSpec as P

MESH = pl.DeviceIdType.MESH
HEAD = 128
HEADS_HERE = 4
CHUNK = 128
CHUNKS = 4
ROWS = CHUNK * CHUNKS
EXTRA = 8
RING_X = 4

NT = (((1,), (1,)), ((), ()))
NN = (((1,), (0,)), ((), ()))
TN = (((0,), (0,)), ((), ()))


def mxu(left, right, form):
    return lax.dot_general(left, right, form, preferred_element_type=jnp.float32)


def split(state):
    high = state.astype(jnp.bfloat16)
    return high, (state - high.astype(jnp.float32)).astype(jnp.bfloat16)


def part(index):
    return slice(index * CHUNK, (index + 1) * CHUNK)


def kernel(
    n_ctx,
    n_dp,
    ring_x,
    q_ref,
    k_ref,
    v_ref,
    decay_ref,
    gain_ref,
    go_ref,
    attended_ref,
    gq_ref,
    gk_ref,
    gv_ref,
    gg_ref,
    rows_ref,
    cols_ref,
    gap_ref,
    weighted_ref,
    gw_ref,
    mix_ref,
    g_ref,
    qw_ref,
    lk_ref,
    lv_ref,
    send_f,
    recv_f,
    back_f,
    start_ref,
    send_b,
    recv_b,
    back_b,
    end_ref,
    sums_ref,
    norm_cols_ref,
    sems_f,
    semr_f,
    sems_fb,
    semr_fb,
    sems_b,
    semr_b,
    sems_bb,
    semr_bb,
    sems_n,
    semr_n,
):
    me = lax.axis_index("ctx")
    col = lax.axis_index("dp")
    piece = ROWS // n_ctx
    per_head = HEAD // piece
    ring_y = n_ctx // ring_x
    my_y, my_x = me // ring_x, me % ring_x

    barrier = pltpu.get_barrier_semaphore()

    def greet_ctx(i, carry):
        pl.semaphore_signal(
            barrier, inc=1, device_id={"ctx": (me + i) % n_ctx}, device_id_type=MESH
        )
        return carry

    def greet_dp(i, carry):
        pl.semaphore_signal(
            barrier, inc=1, device_id={"dp": (col + i) % n_dp}, device_id_type=MESH
        )
        return carry

    lax.fori_loop(1, n_ctx, greet_ctx, 0)
    lax.fori_loop(1, n_dp, greet_dp, 0)

    logs = decay_ref[...]
    stacked = jnp.concatenate([logs[:, part(c)] for c in range(CHUNKS)], axis=0)
    high = stacked.astype(jnp.bfloat16)
    rest = stacked - high.astype(jnp.float32)
    middle = rest.astype(jnp.bfloat16)
    low = (rest - middle.astype(jnp.float32)).astype(jnp.bfloat16)
    row_i = lax.broadcasted_iota(jnp.int32, (CHUNK, 2 * CHUNK), 0)
    col_i = lax.broadcasted_iota(jnp.int32, (CHUNK, 2 * CHUNK), 1)
    adder = jnp.where(row_i <= col_i, 1.0, 0.0).astype(jnp.bfloat16)
    sums = mxu(jnp.concatenate([high, middle, low], axis=0), adder, NN)
    sums = sums[0:16] + sums[16:32] + sums[32:48]
    inside, chunk_total = sums[:, :CHUNK], sums[:, CHUNK:]
    before = jnp.zeros((HEADS_HERE, CHUNK), jnp.float32)
    within = []
    for c in range(CHUNKS):
        block = slice(c * HEADS_HERE, (c + 1) * HEADS_HERE)
        within.append(inside[block] + before)
        before = before + chunk_total[block]
    total = before
    within = jnp.concatenate(within, axis=0)
    tail = jnp.exp(jnp.concatenate([total] * CHUNKS, axis=0) - within)
    rows_ref[...] = within
    cols_ref[...] = jnp.concatenate(
        [within, jnp.exp(within), tail, jnp.zeros((CHUNK - 48, CHUNK), jnp.float32)],
        axis=0,
    ).T

    def column(kind, h, c):
        at = 16 * kind + c * HEADS_HERE + h
        return cols_ref[:, at : at + 1]

    for h in range(HEADS_HERE):
        weighted_keys = jnp.concatenate(
            [
                (k_ref[part(c), part(h)].astype(jnp.float32) * column(2, h, c)).astype(
                    jnp.bfloat16
                )
                for c in range(CHUNKS)
            ],
            axis=0,
        )
        state = mxu(weighted_keys, v_ref[:, part(h)], TN)
        send_f[h * per_head : (h + 1) * per_head, :piece, :] = state.reshape(
            per_head, piece, HEAD
        )
        send_f[h * per_head : (h + 1) * per_head, piece:, :] = jnp.broadcast_to(
            total[h : h + 1][None], (per_head, EXTRA, HEAD)
        )
    recv_f[pl.ds(me, 1)] = send_f[pl.ds(me, 1)]

    pl.semaphore_wait(barrier, n_ctx - 1 + n_dp - 1)

    def far_first(i):
        k, j = i // ring_x, i % ring_x
        step_y = ring_y // 2 + ((k + 1) // 2) * (1 - 2 * ((k + 1) % 2))
        step_x = ring_x // 2 + ((j + 1) // 2) * (1 - 2 * ((j + 1) % 2))
        return ((my_y + step_y) % ring_y) * ring_x + (my_x + step_x) % ring_x

    def out_copy(there, send, recv, ss, rs):
        return pltpu.make_async_remote_copy(
            src_ref=send.at[there],
            dst_ref=recv.at[me],
            send_sem=ss.at[there],
            recv_sem=rs.at[me],
            device_id={"ctx": there},
            device_id_type=MESH,
        )

    def in_copy(there, send, recv, ss, rs):
        return pltpu.make_async_remote_copy(
            src_ref=send.at[there],
            dst_ref=recv.at[there],
            send_sem=ss.at[there],
            recv_sem=rs.at[there],
            device_id={"ctx": there},
            device_id_type=MESH,
        )

    def spread(send, recv, ss, rs):
        def one(i, carry):
            out_copy(far_first(i), send, recv, ss, rs).start()
            return carry

        lax.fori_loop(0, n_ctx - 1, one, 0)

    def wait_sent(send, recv, ss, rs):
        def one(i, carry):
            there = (me + i) % n_ctx
            in_copy(there, send, recv, ss, rs).wait_send()
            return carry

        lax.fori_loop(1, n_ctx, one, 0)

    def wait_pieces(first, last, send, recv, ss, rs):
        def one(there, carry):
            @pl.when(there != me)
            def _():
                in_copy(there, send, recv, ss, rs).wait_recv()

            return carry

        lax.fori_loop(first, last, one, 0)

    spread(send_f, recv_f, sems_f, semr_f)

    diag_t = lax.broadcasted_iota(jnp.int32, (CHUNK, CHUNK), 0)
    diag_s = lax.broadcasted_iota(jnp.int32, (CHUNK, CHUNK), 1)

    def forward_part(h):
        for i in range(CHUNKS):
            scores = mxu(
                q_ref[part(i), part(h)], k_ref[: (i + 1) * CHUNK, part(h)], NT
            )
            here = column(0, h, i)
            for j in range(i + 1):
                at = j * HEADS_HERE + h
                gap = here - rows_ref[at : at + 1, :]
                if i == j:
                    gap = jnp.where(diag_t >= diag_s, gap, -1e30)
                weight = jnp.exp(gap)
                gap_ref[h, part(i), part(j)] = weight
                weighted_ref[h, part(i), part(j)] = (
                    scores[:, part(j)] * weight
                ).astype(jnp.bfloat16)
            mix_ref[part(i), part(h)] = mxu(
                weighted_ref[h, part(i), : (i + 1) * CHUNK],
                v_ref[: (i + 1) * CHUNK, part(h)],
                NN,
            )
            qw_ref[part(i), part(h)] = (
                q_ref[part(i), part(h)].astype(jnp.float32) * column(1, h, i)
            ).astype(jnp.bfloat16)

    forward_part(0)
    forward_part(1)

    def scan_forward(there, running):
        @pl.when(there != me)
        def _():
            in_copy(there, send_f, recv_f, sems_f, semr_f).wait_recv()

        back_f[pl.ds(there, 1)] = running[None]

        @pl.when(there != me)
        def _():
            out_copy(there, back_f, start_ref, sems_fb, semr_fb).start()

        arrived = recv_f[pl.ds(there, 1)][0]
        return jnp.exp(arrived[piece : piece + 1]) * running + arrived[:piece]

    lax.fori_loop(0, n_ctx, scan_forward, jnp.zeros((piece, HEAD), jnp.float32))
    start_ref[pl.ds(me, 1)] = back_f[pl.ds(me, 1)]

    forward_part(2)
    forward_part(3)

    for h in range(HEADS_HERE):
        wait_pieces(
            h * per_head, (h + 1) * per_head, back_f, start_ref, sems_fb, semr_fb
        )
        start = start_ref[h * per_head : (h + 1) * per_head].reshape(HEAD, HEAD)
        high, low = split(start)
        for c in range(CHUNKS):
            rows = q_ref[part(c), part(h)]
            carried = mxu(rows, high, NN) + mxu(rows, low, NN)
            mix_ref[part(c), part(h)] += column(1, h, c) * carried

    ones = jnp.ones((8, CHUNK), jnp.float32)

    def row_sums(terms):
        return lax.dot_general(
            ones,
            terms,
            NT,
            preferred_element_type=jnp.float32,
            precision=lax.Precision.HIGHEST,
        )[0:1]

    squares, crosses = [], []
    for c in range(CHUNKS):
        square = jnp.zeros((CHUNK, HEAD), jnp.float32)
        cross = jnp.zeros((CHUNK, HEAD), jnp.float32)
        for h in range(HEADS_HERE):
            raw = mix_ref[part(c), part(h)]
            square += raw * raw
            cross += (
                go_ref[part(c), part(h)].astype(jnp.float32) * gain_ref[:, part(h)]
            ) * raw
        squares.append(row_sums(square))
        crosses.append(row_sums(cross))
    sums_ref[pl.ds(col, 1)] = jnp.concatenate(squares + crosses, axis=0)[None]

    def norm_copy(slot, there):
        return pltpu.make_async_remote_copy(
            src_ref=sums_ref.at[slot],
            dst_ref=sums_ref.at[slot],
            send_sem=sems_n.at[there],
            recv_sem=semr_n.at[slot],
            device_id={"dp": there},
            device_id_type=MESH,
        )

    def norm_send(i, carry):
        norm_copy(col, (col + n_dp // 2 + i) % n_dp).start()
        return carry

    def norm_wait(i, carry):
        there = (col + i) % n_dp
        norm_copy(there, there).wait_recv()
        return carry

    half = n_dp // 2
    lax.fori_loop(0, half, norm_send, 0)
    lax.fori_loop(half + 1, n_dp, norm_send, 0)
    lax.fori_loop(1, n_dp, norm_wait, 0)

    both = jnp.sum(sums_ref[...], axis=0)
    features = HEAD * HEADS_HERE * n_dp
    inv = lax.rsqrt(both[:CHUNKS] / features + 1e-06)
    bent = inv * inv * inv * both[CHUNKS:] / features
    norm_cols_ref[...] = jnp.concatenate(
        [inv, bent, jnp.zeros((CHUNK - 8, CHUNK), jnp.float32)], axis=0
    ).T

    scale = 1.0 / math.sqrt(ROWS * n_ctx)
    for h in range(HEADS_HERE):
        gain = gain_ref[:, part(h)]
        gain_part = jnp.zeros((1, HEAD), jnp.float32)
        for c in range(CHUNKS):
            raw = mix_ref[part(c), part(h)]
            grad = go_ref[part(c), part(h)].astype(jnp.float32)
            inv_c = norm_cols_ref[:, c : c + 1]
            bent_c = norm_cols_ref[:, CHUNKS + c : CHUNKS + c + 1]
            normed = raw * inv_c
            attended_ref[part(c), part(h)] = (normed * gain).astype(jnp.bfloat16)
            gain_part += jnp.sum(grad * normed, axis=0, keepdims=True)
            g_ref[part(c), part(h)] = (inv_c * (grad * gain) - raw * bent_c).astype(
                jnp.bfloat16
            )
        back = mxu(qw_ref[:, part(h)], g_ref[:, part(h)], TN)
        send_b[h * per_head : (h + 1) * per_head, :piece, :] = back.reshape(
            per_head, piece, HEAD
        )
        send_b[h * per_head : (h + 1) * per_head, piece:, :] = jnp.broadcast_to(
            (gain_part * scale)[None], (per_head, EXTRA, HEAD)
        )
    recv_b[pl.ds(me, 1)] = send_b[pl.ds(me, 1)]
    spread(send_b, recv_b, sems_b, semr_b)

    def backward_part(h):
        start = start_ref[h * per_head : (h + 1) * per_head].reshape(HEAD, HEAD)
        high, low = split(start)
        for i in range(CHUNKS):
            upto = slice(0, (i + 1) * CHUNK)
            rows = g_ref[part(i), part(h)]
            scores = mxu(rows, v_ref[upto, part(h)], NT)
            for j in range(i + 1):
                gw_ref[h, part(i), part(j)] = (
                    scores[:, part(j)] * gap_ref[h, part(i), part(j)]
                ).astype(jnp.bfloat16)
            local = mxu(gw_ref[h, part(i), upto], k_ref[upto, part(h)], NN)
            carried = mxu(rows, high, NT) + mxu(rows, low, NT)
            gq_ref[part(i), part(h)] = (column(1, h, i) * carried + local).astype(
                jnp.bfloat16
            )
        for j in range(CHUNKS):
            down = slice(j * CHUNK, ROWS)
            lk_ref[part(j), part(h)] = mxu(
                gw_ref[h, down, part(j)], q_ref[down, part(h)], TN
            )
            lv_ref[part(j), part(h)] = mxu(
                weighted_ref[h, down, part(j)], g_ref[down, part(h)], TN
            )

    backward_part(0)
    backward_part(1)

    def scan_backward(i, carry):
        running, gain_sum = carry
        there = n_ctx - 1 - i

        @pl.when(there != me)
        def _():
            in_copy(there, send_b, recv_b, sems_b, semr_b).wait_recv()

        back_b[pl.ds(there, 1), :piece] = running[None]
        arrived = recv_b[pl.ds(there, 1)][0]
        decay = jnp.exp(recv_f[pl.ds(there, 1)][0, piece : piece + 1])
        return decay * running + arrived[:piece], gain_sum + arrived[piece:]

    _, gain_sum = lax.fori_loop(
        0,
        n_ctx,
        scan_backward,
        (jnp.zeros((piece, HEAD), jnp.float32), jnp.zeros((EXTRA, HEAD), jnp.float32)),
    )

    def gain_out(there, carry):
        back_b[pl.ds(there, 1), piece:] = gain_sum[None]

        @pl.when(there != me)
        def _():
            out_copy(there, back_b, end_ref, sems_bb, semr_bb).start()

        return carry

    lax.fori_loop(0, n_ctx, gain_out, 0)
    end_ref[pl.ds(me, 1)] = back_b[pl.ds(me, 1)]

    backward_part(2)
    backward_part(3)

    for h in range(HEADS_HERE):
        wait_pieces(
            h * per_head, (h + 1) * per_head, back_b, end_ref, sems_bb, semr_bb
        )
        end = end_ref[h * per_head : (h + 1) * per_head, :piece].reshape(HEAD, HEAD)
        gg_ref[:, part(h)] = end_ref[h * per_head, piece : piece + 1]
        high, low = split(end)
        for c in range(CHUNKS):
            values, keys = v_ref[part(c), part(h)], k_ref[part(c), part(h)]
            fade = column(2, h, c)
            key_carried = mxu(values, high, NT) + mxu(values, low, NT)
            value_carried = mxu(keys, high, NN) + mxu(keys, low, NN)
            gk_ref[part(c), part(h)] = (
                fade * key_carried + lk_ref[part(c), part(h)]
            ).astype(jnp.bfloat16)
            gv_ref[part(c), part(h)] = (
                fade * value_carried + lv_ref[part(c), part(h)]
            ).astype(jnp.bfloat16)

    wait_sent(send_f, recv_f, sems_f, semr_f)
    wait_sent(back_f, start_ref, sems_fb, semr_fb)
    wait_sent(send_b, recv_b, sems_b, semr_b)
    wait_sent(back_b, end_ref, sems_bb, semr_bb)

    def norm_sent(i, carry):
        there = (col + i) % n_dp
        norm_copy(col, there).wait_send()
        return carry

    lax.fori_loop(1, n_dp, norm_sent, 0)


def on_device(
    n_ctx, n_dp, ring_x, query_in, key_in, value_in, log_decay, norm_gain, grad_out
):
    width = HEAD * HEADS_HERE
    piece = ROWS // n_ctx
    full = jax.ShapeDtypeStruct((ROWS, width), jnp.bfloat16)
    f32, bf16 = jnp.float32, jnp.bfloat16
    message = pltpu.VMEM((n_ctx, piece + EXTRA, HEAD), f32)
    plain = pltpu.VMEM((n_ctx, piece, HEAD), f32)
    vmem = pl.BlockSpec(memory_space=pltpu.VMEM)
    outs = pl.pallas_call(
        functools.partial(kernel, n_ctx, n_dp, ring_x),
        out_shape=[full] * 4 + [jax.ShapeDtypeStruct((1, width), f32)],
        in_specs=[vmem] * 6,
        out_specs=[vmem] * 5,
        scratch_shapes=[
            pltpu.VMEM((16, CHUNK), f32),
            pltpu.VMEM((CHUNK, CHUNK), f32),
            pltpu.VMEM((HEADS_HERE, ROWS, ROWS), f32),
            pltpu.VMEM((HEADS_HERE, ROWS, ROWS), bf16),
            pltpu.VMEM((HEADS_HERE, ROWS, ROWS), bf16),
            pltpu.VMEM((ROWS, width), f32),
            pltpu.VMEM((ROWS, width), bf16),
            pltpu.VMEM((ROWS, width), bf16),
            pltpu.VMEM((ROWS, width), f32),
            pltpu.VMEM((ROWS, width), f32),
            message,
            message,
            plain,
            plain,
            message,
            message,
            message,
            message,
            pltpu.VMEM((n_dp, 8, CHUNK), f32),
            pltpu.VMEM((CHUNK, CHUNK), f32),
        ]
        + [pltpu.SemaphoreType.DMA((n_ctx,))] * 8
        + [pltpu.SemaphoreType.DMA((n_dp,))] * 2,
        compiler_params=pltpu.CompilerParams(
            collective_id=0,
            has_side_effects=True,
            vmem_limit_bytes=40 * 1024 * 1024,
        ),
        name="lightning",
    )(
        query_in,
        key_in,
        value_in,
        log_decay,
        norm_gain.reshape(1, width),
        grad_out,
    )
    return (*outs[:4], outs[4].reshape(width))


def solution(mesh):
    in_specs = (
        P("ctx", "dp"),
        P("ctx", "dp"),
        P("ctx", "dp"),
        P("dp", "ctx"),
        P("dp"),
        P("ctx", "dp"),
    )
    out_specs = (P("ctx", "dp"), P("ctx", "dp"), P("ctx", "dp"), P("ctx", "dp"), P("dp"))
    n_ctx, n_dp = mesh.shape["ctx"], mesh.shape["dp"]
    return jax.shard_map(
        functools.partial(on_device, n_ctx, n_dp, min(RING_X, n_ctx // 2)),
        mesh=mesh,
        in_specs=in_specs,
        out_specs=out_specs,
        check_vma=False,
    )
```

```python
import functools
import math

import jax
import jax.numpy as jnp
from jax import lax
from jax.experimental import pallas as pl
from jax.experimental.pallas import tpu as pltpu
from jax.sharding import PartitionSpec as P

MESH = pl.DeviceIdType.MESH
HEAD = 128
HEADS_HERE = 4
CHUNK = 128
CHUNKS = 4
ROWS = CHUNK * CHUNKS
EXTRA = 8
RING_X = 4
VMEM_BYTES = 48 * 1024 * 1024

NT = (((1,), (1,)), ((), ()))
NN = (((1,), (0,)), ((), ()))
TN = (((0,), (0,)), ((), ()))


def mxu(left, right, form):
    return lax.dot_general(left, right, form, preferred_element_type=jnp.float32)


def split(state):
    high = state.astype(jnp.bfloat16)
    return high, (state - high.astype(jnp.float32)).astype(jnp.bfloat16)


def part(index):
    return slice(index * CHUNK, (index + 1) * CHUNK)


def kernel(
    n_ctx,
    n_dp,
    ring_x,
    q_hbm,
    k_hbm,
    v_hbm,
    decay_hbm,
    gain_hbm,
    go_hbm,
    attended_ref,
    gq_ref,
    gk_ref,
    gv_ref,
    gg_ref,
    q_ref,
    k_ref,
    v_ref,
    decay_ref,
    gain_ref,
    go_ref,
    sem_in,
    rows_ref,
    cols_ref,
    gap_ref,
    weighted_ref,
    gw_ref,
    mix_ref,
    g_ref,
    qw_ref,
    lk_ref,
    lv_ref,
    send_f,
    recv_f,
    back_f,
    start_ref,
    send_b,
    recv_b,
    back_b,
    end_ref,
    gain_out,
    gain_in,
    sums_ref,
    norm_cols_ref,
    sems_f,
    semr_f,
    sems_fb,
    semr_fb,
    sems_b,
    semr_b,
    sems_bb,
    semr_bb,
    sems_n,
    semr_n,
    sems_g,
    semr_g,
):
    me = lax.axis_index("ctx")
    col = lax.axis_index("dp")
    piece = ROWS // n_ctx
    per_head = HEAD // piece
    ring_y = n_ctx // ring_x
    my_y, my_x = me // ring_x, me % ring_x
    my_head = me // per_head
    ring_z = n_dp // 2
    far_x = sorted(range(ring_x), key=lambda d: -min(d, ring_x - d))

    loads = [
        pltpu.make_async_copy(source, target, sem_in.at[i])
        for i, (source, target) in enumerate(
            (
                (decay_hbm, decay_ref),
                (k_hbm, k_ref),
                (v_hbm, v_ref),
                (q_hbm, q_ref),
                (gain_hbm, gain_ref),
                (go_hbm, go_ref),
            )
        )
    ]
    for load in loads:
        load.start()
    barrier = pltpu.get_barrier_semaphore()

    def far_line(i):
        step = ring_y // 2 + ((i + 1) // 2) * (1 - 2 * ((i + 1) % 2))
        return ((my_y + step) % ring_y) * ring_x

    def greet(there):
        pl.semaphore_signal(
            barrier, inc=1, device_id={"ctx": there}, device_id_type=MESH
        )

    def greet_line(i, carry):
        line = far_line(i)
        for step_x in far_x:
            greet(line + (my_x + step_x) % ring_x)
        return carry

    lax.fori_loop(0, ring_y - 1, greet_line, 0)
    for step_x in far_x[:-1]:
        greet(my_y * ring_x + (my_x + step_x) % ring_x)

    def greet_dp(i, carry):
        pl.semaphore_signal(
            barrier, inc=1, device_id={"dp": (col + i) % n_dp}, device_id_type=MESH
        )
        return carry

    lax.fori_loop(1, n_dp, greet_dp, 0)

    loads[0].wait()
    logs = decay_ref[...]
    stacked = jnp.concatenate([logs[:, part(c)] for c in range(CHUNKS)], axis=0)
    high = stacked.astype(jnp.bfloat16)
    rest = stacked - high.astype(jnp.float32)
    middle = rest.astype(jnp.bfloat16)
    low = (rest - middle.astype(jnp.float32)).astype(jnp.bfloat16)
    row_i = lax.broadcasted_iota(jnp.int32, (CHUNK, 2 * CHUNK), 0)
    col_i = lax.broadcasted_iota(jnp.int32, (CHUNK, 2 * CHUNK), 1)
    adder = jnp.where(row_i <= col_i, 1.0, 0.0).astype(jnp.bfloat16)
    sums = mxu(jnp.concatenate([high, middle, low], axis=0), adder, NN)
    sums = sums[0:16] + sums[16:32] + sums[32:48]
    inside, chunk_total = sums[:, :CHUNK], sums[:, CHUNK:]
    before = jnp.zeros((HEADS_HERE, CHUNK), jnp.float32)
    within = []
    for c in range(CHUNKS):
        block = slice(c * HEADS_HERE, (c + 1) * HEADS_HERE)
        within.append(inside[block] + before)
        before = before + chunk_total[block]
    total = before
    within = jnp.concatenate(within, axis=0)
    tail = jnp.exp(jnp.concatenate([total] * CHUNKS, axis=0) - within)
    rows_ref[...] = within
    cols_ref[...] = jnp.concatenate(
        [within, jnp.exp(within), tail, jnp.zeros((CHUNK - 48, CHUNK), jnp.float32)],
        axis=0,
    ).T

    def column(kind, h, c):
        at = 16 * kind + c * HEADS_HERE + h
        return cols_ref[:, at : at + 1]

    loads[1].wait()
    loads[2].wait()

    for h in range(HEADS_HERE):
        weighted_keys = jnp.concatenate(
            [
                (k_ref[part(c), part(h)].astype(jnp.float32) * column(2, h, c)).astype(
                    jnp.bfloat16
                )
                for c in range(CHUNKS)
            ],
            axis=0,
        )
        state = mxu(weighted_keys, v_ref[:, part(h)], TN)
        send_f[h * per_head : (h + 1) * per_head, :piece, :] = state.reshape(
            per_head, piece, HEAD
        )
        send_f[h * per_head : (h + 1) * per_head, piece:, :] = jnp.broadcast_to(
            total[h : h + 1][None], (per_head, EXTRA, HEAD)
        )
    pl.semaphore_wait(barrier, n_ctx - 1 + n_dp - 1)

    taken, given = pl.ds(0, piece + 1), pl.ds(0, piece)

    def copy_to(there, rows, source, target, ss, rs):
        return pltpu.make_async_remote_copy(
            src_ref=source.at[there, rows],
            dst_ref=target.at[me, rows],
            send_sem=ss,
            recv_sem=rs,
            device_id={"ctx": there},
            device_id_type=MESH,
        )

    def own_copy(rows, source, target, rs):
        return pltpu.make_async_copy(source.at[me, rows], target.at[me, rows], rs)

    def wait_group(first, count, rows, source, target, rs):
        group = pl.ds(first, count)
        pltpu.make_async_copy(
            source.at[group, rows], target.at[group, rows], rs
        ).wait()

    def spread(source, target, ss, rs):
        own_copy(taken, source, target, rs.at[my_y]).start()

        def one(i, carry):
            line = far_line(i)
            for step_x in far_x:
                there = line + (my_x + step_x) % ring_x
                copy_to(there, taken, source, target, ss, rs.at[my_y]).start()
            return carry

        lax.fori_loop(0, ring_y - 1, one, 0)
        for step_x in far_x[:-1]:
            there = my_y * ring_x + (my_x + step_x) % ring_x
            copy_to(there, taken, source, target, ss, rs.at[my_y]).start()

    def give_back(there, running, source, target, ss, rs):
        source[pl.ds(there, 1)] = running[None]

        @pl.when(there != me)
        def _():
            copy_to(there, given, source, target, ss, rs.at[my_head]).start()

        @pl.when(there == me)
        def _():
            own_copy(given, source, target, rs.at[my_head]).start()

    spread(send_f, recv_f, sems_f, semr_f)

    for load in loads[3:]:
        load.wait()

    diag_t = lax.broadcasted_iota(jnp.int32, (CHUNK, CHUNK), 0)
    diag_s = lax.broadcasted_iota(jnp.int32, (CHUNK, CHUNK), 1)

    def forward_part(h):
        for i in range(CHUNKS):
            scores = mxu(
                q_ref[part(i), part(h)], k_ref[: (i + 1) * CHUNK, part(h)], NT
            )
            here = column(0, h, i)
            for j in range(i + 1):
                at = j * HEADS_HERE + h
                gap = here - rows_ref[at : at + 1, :]
                if i == j:
                    gap = jnp.where(diag_t >= diag_s, gap, -1e30)
                weight = jnp.exp(gap)
                gap_ref[h, part(i), part(j)] = weight
                weighted_ref[h, part(i), part(j)] = (
                    scores[:, part(j)] * weight
                ).astype(jnp.bfloat16)
            mix_ref[part(i), part(h)] = mxu(
                weighted_ref[h, part(i), : (i + 1) * CHUNK],
                v_ref[: (i + 1) * CHUNK, part(h)],
                NN,
            )
            qw_ref[part(i), part(h)] = (
                q_ref[part(i), part(h)].astype(jnp.float32) * column(1, h, i)
            ).astype(jnp.bfloat16)

    forward_part(0)
    forward_part(1)

    def scan_forward(line, running):
        first = line * ring_x
        wait_group(first, ring_x, taken, send_f, recv_f, semr_f.at[line])
        for x in range(ring_x):
            there = first + x
            give_back(there, running, back_f, start_ref, sems_fb, semr_fb)
            arrived = recv_f[pl.ds(there, 1)][0]
            running = jnp.exp(arrived[piece : piece + 1]) * running + arrived[:piece]
        return running

    lax.fori_loop(0, ring_y, scan_forward, jnp.zeros((piece, HEAD), jnp.float32))

    forward_part(2)
    forward_part(3)

    for h in range(HEADS_HERE):
        wait_group(
            h * per_head, per_head, given, back_f, start_ref, semr_fb.at[h]
        )
        start = start_ref[h * per_head : (h + 1) * per_head].reshape(HEAD, HEAD)
        high, low = split(start)
        for c in range(CHUNKS):
            rows = q_ref[part(c), part(h)]
            carried = mxu(rows, high, NN) + mxu(rows, low, NN)
            mix_ref[part(c), part(h)] += column(1, h, c) * carried

    ones = jnp.ones((8, CHUNK), jnp.float32)

    def row_sums(terms):
        return lax.dot_general(
            ones,
            terms,
            NT,
            preferred_element_type=jnp.float32,
            precision=lax.Precision.HIGHEST,
        )[0:1]

    squares, crosses = [], []
    for c in range(CHUNKS):
        square = jnp.zeros((CHUNK, HEAD), jnp.float32)
        cross = jnp.zeros((CHUNK, HEAD), jnp.float32)
        for h in range(HEADS_HERE):
            raw = mix_ref[part(c), part(h)]
            square += raw * raw
            cross += (
                go_ref[part(c), part(h)].astype(jnp.float32) * gain_ref[:, part(h)]
            ) * raw
        squares.append(row_sums(square))
        crosses.append(row_sums(cross))
    sums_ref[pl.ds(col, 1)] = jnp.concatenate(squares + crosses, axis=0)[None]

    def norm_copy(slot, there):
        return pltpu.make_async_remote_copy(
            src_ref=sums_ref.at[slot],
            dst_ref=sums_ref.at[slot],
            send_sem=sems_n,
            recv_sem=semr_n,
            device_id={"dp": there},
            device_id_type=MESH,
        )

    def norm_send(i, carry):
        step = ring_z // 2 + ((i + 1) // 2) * (1 - 2 * ((i + 1) % 2))
        level = ((col // 2 + step) % ring_z) * 2
        for core in range(2):
            norm_copy(col, level + core).start()
        return carry

    lax.fori_loop(0, ring_z - 1, norm_send, 0)
    norm_copy(col, col + 1 - 2 * (col % 2)).start()
    pltpu.make_async_copy(
        sums_ref.at[pl.ds(0, n_dp - 1)], sums_ref.at[pl.ds(0, n_dp - 1)], semr_n
    ).wait()

    both = jnp.sum(sums_ref[...], axis=0)
    features = HEAD * HEADS_HERE * n_dp
    inv = lax.rsqrt(both[:CHUNKS] / features + 1e-06)
    bent = inv * inv * inv * both[CHUNKS:] / features
    norm_cols_ref[...] = jnp.concatenate(
        [inv, bent, jnp.zeros((CHUNK - 8, CHUNK), jnp.float32)], axis=0
    ).T

    scale = 1.0 / math.sqrt(ROWS * n_ctx)
    for h in range(HEADS_HERE):
        gain = gain_ref[:, part(h)]
        gain_part = jnp.zeros((1, HEAD), jnp.float32)
        for c in range(CHUNKS):
            raw = mix_ref[part(c), part(h)]
            grad = go_ref[part(c), part(h)].astype(jnp.float32)
            inv_c = norm_cols_ref[:, c : c + 1]
            bent_c = norm_cols_ref[:, CHUNKS + c : CHUNKS + c + 1]
            normed = raw * inv_c
            attended_ref[part(c), part(h)] = (normed * gain).astype(jnp.bfloat16)
            gain_part += jnp.sum(grad * normed, axis=0, keepdims=True)
            g_ref[part(c), part(h)] = (inv_c * (grad * gain) - raw * bent_c).astype(
                jnp.bfloat16
            )
        back = mxu(qw_ref[:, part(h)], g_ref[:, part(h)], TN)
        send_b[h * per_head : (h + 1) * per_head, :piece, :] = back.reshape(
            per_head, piece, HEAD
        )
        send_b[h * per_head : (h + 1) * per_head, piece:, :] = jnp.broadcast_to(
            (gain_part * scale)[None], (per_head, EXTRA, HEAD)
        )
    spread(send_b, recv_b, sems_b, semr_b)

    def backward_part(h):
        start = start_ref[h * per_head : (h + 1) * per_head].reshape(HEAD, HEAD)
        high, low = split(start)
        for i in range(CHUNKS):
            upto = slice(0, (i + 1) * CHUNK)
            rows = g_ref[part(i), part(h)]
            scores = mxu(rows, v_ref[upto, part(h)], NT)
            for j in range(i + 1):
                gw_ref[h, part(i), part(j)] = (
                    scores[:, part(j)] * gap_ref[h, part(i), part(j)]
                ).astype(jnp.bfloat16)
            local = mxu(gw_ref[h, part(i), upto], k_ref[upto, part(h)], NN)
            carried = mxu(rows, high, NT) + mxu(rows, low, NT)
            gq_ref[part(i), part(h)] = (column(1, h, i) * carried + local).astype(
                jnp.bfloat16
            )
        for j in range(CHUNKS):
            down = slice(j * CHUNK, ROWS)
            lk_ref[part(j), part(h)] = mxu(
                gw_ref[h, down, part(j)], q_ref[down, part(h)], TN
            )
            lv_ref[part(j), part(h)] = mxu(
                weighted_ref[h, down, part(j)], g_ref[down, part(h)], TN
            )

    backward_part(0)
    backward_part(1)

    def scan_backward(i, carry):
        running, gain_sum = carry
        line = ring_y - 1 - i
        first = line * ring_x
        wait_group(first, ring_x, taken, send_b, recv_b, semr_b.at[line])
        for x in reversed(range(ring_x)):
            there = first + x
            give_back(there, running, back_b, end_ref, sems_bb, semr_bb)
            arrived = recv_b[pl.ds(there, 1)][0]
            decay = jnp.exp(recv_f[pl.ds(there, 1)][0, piece : piece + 1])
            running = decay * running + arrived[:piece]
            gain_sum = gain_sum + arrived[piece : piece + 1]
        return running, gain_sum

    nothing = jnp.zeros((1, HEAD), jnp.float32)
    _, gain_sum = lax.fori_loop(
        0, ring_y, scan_backward, (jnp.zeros((piece, HEAD), jnp.float32), nothing)
    )

    one_row = pl.ds(0, 1)

    @pl.when(me % per_head == 0)
    def _():
        gain_out[...] = jnp.broadcast_to(gain_sum, (8, HEAD))
        pltpu.make_async_copy(
            gain_out.at[one_row], gain_in.at[my_head, one_row], semr_g
        ).start()

        def tell(i, carry):
            pltpu.make_async_remote_copy(
                src_ref=gain_out.at[one_row],
                dst_ref=gain_in.at[my_head, one_row],
                send_sem=sems_g,
                recv_sem=semr_g,
                device_id={"ctx": (me + n_ctx // 2 + i) % n_ctx},
                device_id_type=MESH,
            ).start()
            return carry

        lax.fori_loop(0, n_ctx // 2, tell, 0)
        lax.fori_loop(n_ctx // 2 + 1, n_ctx, tell, 0)

    backward_part(2)
    backward_part(3)

    for h in range(HEADS_HERE):
        wait_group(
            h * per_head, per_head, given, back_b, end_ref, semr_bb.at[h]
        )
        end = end_ref[h * per_head : (h + 1) * per_head].reshape(HEAD, HEAD)
        high, low = split(end)
        for c in range(CHUNKS):
            values, keys = v_ref[part(c), part(h)], k_ref[part(c), part(h)]
            fade = column(2, h, c)
            key_carried = mxu(values, high, NT) + mxu(values, low, NT)
            value_carried = mxu(keys, high, NN) + mxu(keys, low, NN)
            gk_ref[part(c), part(h)] = (
                fade * key_carried + lk_ref[part(c), part(h)]
            ).astype(jnp.bfloat16)
            gv_ref[part(c), part(h)] = (
                fade * value_carried + lv_ref[part(c), part(h)]
            ).astype(jnp.bfloat16)

    pltpu.make_async_copy(
        gain_in.at[:, one_row], gain_in.at[:, one_row], semr_g
    ).wait()
    for h in range(HEADS_HERE):
        gg_ref[:, part(h)] = gain_in[h, 0:1]

    @pl.when(me % per_head == 0)
    def _():
        pltpu.make_async_copy(
            recv_f.at[pl.ds(0, n_ctx - 1), one_row],
            recv_b.at[pl.ds(0, n_ctx - 1), one_row],
            sems_g,
        ).wait()

    wait_group(0, n_ctx - 1, taken, send_f, recv_f, sems_f)
    wait_group(0, n_ctx - 1, given, back_f, start_ref, sems_fb)
    wait_group(0, n_ctx - 1, taken, send_b, recv_b, sems_b)
    wait_group(0, n_ctx - 1, given, back_b, end_ref, sems_bb)
    pltpu.make_async_copy(
        sums_ref.at[pl.ds(0, n_dp - 1)], sums_ref.at[pl.ds(0, n_dp - 1)], sems_n
    ).wait()


def store(*refs):
    count = len(refs) // 2
    sems = refs[-1]
    copies = [
        pltpu.make_async_copy(refs[i], refs[count + i], sems.at[i])
        for i in range(count)
    ]
    for copy in copies:
        copy.start()
    for copy in copies:
        copy.wait()


def on_device(
    n_ctx, n_dp, ring_x, query_in, key_in, value_in, log_decay, norm_gain, grad_out
):
    width = HEAD * HEADS_HERE
    piece = ROWS // n_ctx
    full = jax.ShapeDtypeStruct((ROWS, width), jnp.bfloat16)
    f32, bf16 = jnp.float32, jnp.bfloat16
    message = pltpu.VMEM((n_ctx, piece + EXTRA, HEAD), f32)
    plain = pltpu.VMEM((n_ctx, piece, HEAD), f32)
    vmem = pl.BlockSpec(memory_space=pltpu.VMEM)
    hbm = pl.BlockSpec(memory_space=pltpu.HBM)
    outs = pl.pallas_call(
        functools.partial(kernel, n_ctx, n_dp, ring_x),
        out_shape=[full] * 4 + [jax.ShapeDtypeStruct((1, width), f32)],
        in_specs=[hbm] * 6,
        out_specs=[vmem] * 5,
        scratch_shapes=[
            pltpu.VMEM((ROWS, width), bf16),
            pltpu.VMEM((ROWS, width), bf16),
            pltpu.VMEM((ROWS, width), bf16),
            pltpu.VMEM((HEADS_HERE, ROWS), f32),
            pltpu.VMEM((1, width), f32),
            pltpu.VMEM((ROWS, width), bf16),
            pltpu.SemaphoreType.DMA((6,)),
            pltpu.VMEM((16, CHUNK), f32),
            pltpu.VMEM((CHUNK, CHUNK), f32),
            pltpu.VMEM((HEADS_HERE, ROWS, ROWS), f32),
            pltpu.VMEM((HEADS_HERE, ROWS, ROWS), bf16),
            pltpu.VMEM((HEADS_HERE, ROWS, ROWS), bf16),
            pltpu.VMEM((ROWS, width), f32),
            pltpu.VMEM((ROWS, width), bf16),
            pltpu.VMEM((ROWS, width), bf16),
            pltpu.VMEM((ROWS, width), f32),
            pltpu.VMEM((ROWS, width), f32),
            message,
            message,
            plain,
            plain,
            message,
            message,
            plain,
            plain,
            pltpu.VMEM((8, HEAD), f32),
            pltpu.VMEM((HEADS_HERE, 8, HEAD), f32),
            pltpu.VMEM((n_dp, 8, CHUNK), f32),
            pltpu.VMEM((CHUNK, CHUNK), f32),
        ]
        + [
            pltpu.SemaphoreType.DMA,
            pltpu.SemaphoreType.DMA((n_ctx // ring_x,)),
            pltpu.SemaphoreType.DMA,
            pltpu.SemaphoreType.DMA((HEADS_HERE,)),
        ]
        * 2
        + [pltpu.SemaphoreType.DMA] * 4,
        compiler_params=pltpu.CompilerParams(
            collective_id=0,
            has_side_effects=True,
            vmem_limit_bytes=VMEM_BYTES,
        ),
        name="lightning",
    )(
        *(
            pltpu.with_memory_space_constraint(array, pltpu.HBM)
            for array in (
                query_in,
                key_in,
                value_in,
                log_decay,
                norm_gain.reshape(1, width),
                grad_out,
            )
        )
    )
    stored = pl.pallas_call(
        store,
        out_shape=[full] * 4 + [jax.ShapeDtypeStruct((1, width), f32)],
        in_specs=[vmem] * 5,
        out_specs=[hbm] * 5,
        scratch_shapes=[pltpu.SemaphoreType.DMA((5,))],
        compiler_params=pltpu.CompilerParams(vmem_limit_bytes=1024 * 1024),
        name="store",
    )(*outs)
    return (*stored[:4], stored[4].reshape(width))


def solution(mesh):
    in_specs = (
        P("ctx", "dp"),
        P("ctx", "dp"),
        P("ctx", "dp"),
        P("dp", "ctx"),
        P("dp"),
        P("ctx", "dp"),
    )
    out_specs = (P("ctx", "dp"), P("ctx", "dp"), P("ctx", "dp"), P("ctx", "dp"), P("dp"))
    n_ctx, n_dp = mesh.shape["ctx"], mesh.shape["dp"]
    return jax.shard_map(
        functools.partial(on_device, n_ctx, n_dp, min(RING_X, n_ctx // 2)),
        mesh=mesh,
        in_specs=in_specs,
        out_specs=out_specs,
        check_vma=False,
    )
```

```python
import functools
import math

import jax
import jax.numpy as jnp
from jax import lax
from jax.experimental import pallas as pl
from jax.experimental.pallas import tpu as pltpu
from jax.sharding import PartitionSpec as P

MESH = pl.DeviceIdType.MESH
HEAD = 128
HEADS_HERE = 4
CHUNK = 128
CHUNKS = 4
ROWS = CHUNK * CHUNKS
EXTRA = 8
RING_X = 4
VMEM_BYTES = 48 * 1024 * 1024

NT = (((1,), (1,)), ((), ()))
NN = (((1,), (0,)), ((), ()))
TN = (((0,), (0,)), ((), ()))


def mxu(left, right, form):
    return lax.dot_general(left, right, form, preferred_element_type=jnp.float32)


def part(index):
    return slice(index * CHUNK, (index + 1) * CHUNK)


def kernel(
    n_ctx,
    n_dp,
    ring_x,
    q_hbm,
    k_hbm,
    v_hbm,
    decay_hbm,
    gain_hbm,
    go_hbm,
    attended_ref,
    gq_ref,
    gg_ref,
    k_ref,
    v_ref,
    cols_ref,
    lk_ref,
    lv_ref,
    end_ref,
    q_ref,
    decay_ref,
    gain_ref,
    go_ref,
    sem_in,
    rows_ref,
    gap_ref,
    weighted_ref,
    gw_ref,
    mix_ref,
    g_ref,
    qw_ref,
    send_f,
    recv_f,
    back_f,
    start_ref,
    send_b,
    recv_b,
    back_b,
    gain_out,
    gain_in,
    sums_ref,
    norm_cols_ref,
    sems_f,
    semr_f,
    sems_fb,
    semr_fb,
    sems_b,
    semr_b,
    sems_bb,
    semr_bb,
    sems_n,
    semr_n,
    sems_g,
    semr_g,
):
    me = lax.axis_index("ctx")
    col = lax.axis_index("dp")
    piece = ROWS // n_ctx
    per_head = HEAD // piece
    ring_y = n_ctx // ring_x
    my_y, my_x = me // ring_x, me % ring_x
    my_head = me // per_head
    ring_z = n_dp // 2
    far_x = sorted(range(ring_x), key=lambda d: -min(d, ring_x - d))

    loads = [
        pltpu.make_async_copy(source, target, sem_in.at[i])
        for i, (source, target) in enumerate(
            (
                (decay_hbm, decay_ref),
                (k_hbm, k_ref),
                (v_hbm, v_ref),
                (q_hbm, q_ref),
                (gain_hbm, gain_ref),
                (go_hbm, go_ref),
            )
        )
    ]
    for load in loads:
        load.start()
    barrier = pltpu.get_barrier_semaphore()

    def far_line(i):
        step = ring_y // 2 + ((i + 1) // 2) * (1 - 2 * ((i + 1) % 2))
        return ((my_y + step) % ring_y) * ring_x

    def greet(there):
        pl.semaphore_signal(
            barrier, inc=1, device_id={"ctx": there}, device_id_type=MESH
        )

    def greet_line(i, carry):
        line = far_line(i)
        for step_x in far_x:
            greet(line + (my_x + step_x) % ring_x)
        return carry

    lax.fori_loop(0, ring_y - 1, greet_line, 0)
    for step_x in far_x[:-1]:
        greet(my_y * ring_x + (my_x + step_x) % ring_x)

    def greet_dp(i, carry):
        pl.semaphore_signal(
            barrier, inc=1, device_id={"dp": (col + i) % n_dp}, device_id_type=MESH
        )
        return carry

    lax.fori_loop(1, n_dp, greet_dp, 0)

    loads[0].wait()
    logs = decay_ref[...]
    stacked = jnp.concatenate([logs[:, part(c)] for c in range(CHUNKS)], axis=0)
    high = stacked.astype(jnp.bfloat16)
    rest = stacked - high.astype(jnp.float32)
    middle = rest.astype(jnp.bfloat16)
    low = (rest - middle.astype(jnp.float32)).astype(jnp.bfloat16)
    row_i = lax.broadcasted_iota(jnp.int32, (CHUNK, 2 * CHUNK), 0)
    col_i = lax.broadcasted_iota(jnp.int32, (CHUNK, 2 * CHUNK), 1)
    adder = jnp.where(row_i <= col_i, 1.0, 0.0).astype(jnp.bfloat16)
    sums = mxu(jnp.concatenate([high, middle, low], axis=0), adder, NN)
    sums = sums[0:16] + sums[16:32] + sums[32:48]
    inside, chunk_total = sums[:, :CHUNK], sums[:, CHUNK:]
    before = jnp.zeros((HEADS_HERE, CHUNK), jnp.float32)
    within = []
    for c in range(CHUNKS):
        block = slice(c * HEADS_HERE, (c + 1) * HEADS_HERE)
        within.append(inside[block] + before)
        before = before + chunk_total[block]
    total = before
    within = jnp.concatenate(within, axis=0)
    tail = jnp.exp(jnp.concatenate([total] * CHUNKS, axis=0) - within)
    rows_ref[...] = within
    cols_ref[...] = jnp.concatenate(
        [within, jnp.exp(within), tail, jnp.zeros((CHUNK - 48, CHUNK), jnp.float32)],
        axis=0,
    ).T

    def column(kind, h, c):
        at = 16 * kind + c * HEADS_HERE + h
        return cols_ref[:, at : at + 1]

    loads[1].wait()
    loads[2].wait()

    for h in range(HEADS_HERE):
        weighted_keys = jnp.concatenate(
            [
                (k_ref[part(c), part(h)].astype(jnp.float32) * column(2, h, c)).astype(
                    jnp.bfloat16
                )
                for c in range(CHUNKS)
            ],
            axis=0,
        )
        state = mxu(weighted_keys, v_ref[:, part(h)], TN)
        send_f[h * per_head : (h + 1) * per_head, :piece, :] = state.reshape(
            per_head, piece, HEAD
        )
        send_f[h * per_head : (h + 1) * per_head, piece:, :] = jnp.broadcast_to(
            total[h : h + 1][None], (per_head, EXTRA, HEAD)
        )
    pl.semaphore_wait(barrier, n_ctx - 1 + n_dp - 1)

    taken, given = pl.ds(0, piece + 1), pl.ds(0, piece)

    def copy_to(there, rows, source, target, ss, rs):
        return pltpu.make_async_remote_copy(
            src_ref=source.at[there, rows],
            dst_ref=target.at[me, rows],
            send_sem=ss,
            recv_sem=rs,
            device_id={"ctx": there},
            device_id_type=MESH,
        )

    def own_copy(rows, source, target, rs):
        return pltpu.make_async_copy(source.at[me, rows], target.at[me, rows], rs)

    def wait_group(first, count, rows, source, target, rs):
        group = pl.ds(first, count)
        pltpu.make_async_copy(
            source.at[group, rows], target.at[group, rows], rs
        ).wait()

    def spread(source, target, ss, rs):
        own_copy(taken, source, target, rs.at[my_y]).start()

        def one(i, carry):
            line = far_line(i)
            for step_x in far_x:
                there = line + (my_x + step_x) % ring_x
                copy_to(there, taken, source, target, ss, rs.at[my_y]).start()
            return carry

        lax.fori_loop(0, ring_y - 1, one, 0)
        for step_x in far_x[:-1]:
            there = my_y * ring_x + (my_x + step_x) % ring_x
            copy_to(there, taken, source, target, ss, rs.at[my_y]).start()

    def spread_head(h, source, target, ss, rs):
        def one(there, carry):
            @pl.when(there != me)
            def _():
                copy_to(there, taken, source, target, ss, rs.at[my_y]).start()

            @pl.when(there == me)
            def _():
                own_copy(taken, source, target, rs.at[my_y]).start()

            return carry

        lax.fori_loop(h * per_head, (h + 1) * per_head, one, 0)

    def give_back(there, running, source, target, ss, rs):
        source[pl.ds(there, 1)] = running[None]

        @pl.when(there != me)
        def _():
            copy_to(there, given, source, target, ss, rs.at[my_head]).start()

        @pl.when(there == me)
        def _():
            own_copy(given, source, target, rs.at[my_head]).start()

    spread(send_f, recv_f, sems_f, semr_f)

    for load in loads[3:]:
        load.wait()

    diag_t = lax.broadcasted_iota(jnp.int32, (CHUNK, CHUNK), 0)
    diag_s = lax.broadcasted_iota(jnp.int32, (CHUNK, CHUNK), 1)

    def forward_part(h):
        for i in range(CHUNKS):
            scores = mxu(
                q_ref[part(i), part(h)], k_ref[: (i + 1) * CHUNK, part(h)], NT
            )
            here = column(0, h, i)
            for j in range(i + 1):
                at = j * HEADS_HERE + h
                gap = here - rows_ref[at : at + 1, :]
                if i == j:
                    gap = jnp.where(diag_t >= diag_s, gap, -1e30)
                weight = jnp.exp(gap)
                gap_ref[h, part(i), part(j)] = weight
                weighted_ref[h, part(i), part(j)] = (
                    scores[:, part(j)] * weight
                ).astype(jnp.bfloat16)
            mix_ref[part(i), part(h)] = mxu(
                weighted_ref[h, part(i), : (i + 1) * CHUNK],
                v_ref[: (i + 1) * CHUNK, part(h)],
                NN,
            )
            qw_ref[part(h), part(i)] = (
                (q_ref[part(i), part(h)].astype(jnp.float32) * column(1, h, i)).T
            ).astype(jnp.bfloat16)

    forward_part(0)

    def scan_forward(line, running):
        first = line * ring_x
        wait_group(first, ring_x, taken, send_f, recv_f, semr_f.at[line])
        for x in range(ring_x):
            there = first + x
            give_back(there, running, back_f, start_ref, sems_fb, semr_fb)
            arrived = recv_f[pl.ds(there, 1)][0]
            running = jnp.exp(arrived[piece : piece + 1]) * running + arrived[:piece]
        return running

    lax.fori_loop(0, ring_y, scan_forward, jnp.zeros((piece, HEAD), jnp.float32))

    forward_part(1)
    forward_part(2)
    forward_part(3)

    for h in range(HEADS_HERE):
        wait_group(
            h * per_head, per_head, given, back_f, start_ref, semr_fb.at[h]
        )
        start = start_ref[h * per_head : (h + 1) * per_head].reshape(HEAD, HEAD)
        start = start.astype(jnp.bfloat16)
        for c in range(CHUNKS):
            carried = mxu(q_ref[part(c), part(h)], start, NN)
            mix_ref[part(c), part(h)] += column(1, h, c) * carried

    ones = jnp.ones((8, CHUNK), jnp.float32)

    def row_sums(terms):
        return lax.dot_general(
            ones,
            terms,
            NT,
            preferred_element_type=jnp.float32,
            precision=lax.Precision.HIGHEST,
        )[0:1]

    squares, crosses = [], []
    for c in range(CHUNKS):
        square = jnp.zeros((CHUNK, HEAD), jnp.float32)
        cross = jnp.zeros((CHUNK, HEAD), jnp.float32)
        for h in range(HEADS_HERE):
            raw = mix_ref[part(c), part(h)]
            square += raw * raw
            cross += (
                go_ref[part(c), part(h)].astype(jnp.float32) * gain_ref[:, part(h)]
            ) * raw
        squares.append(row_sums(square))
        crosses.append(row_sums(cross))
    sums_ref[pl.ds(col, 1)] = jnp.concatenate(squares + crosses, axis=0)[None]

    def norm_copy(slot, there):
        return pltpu.make_async_remote_copy(
            src_ref=sums_ref.at[slot],
            dst_ref=sums_ref.at[slot],
            send_sem=sems_n,
            recv_sem=semr_n,
            device_id={"dp": there},
            device_id_type=MESH,
        )

    def norm_send(i, carry):
        step = ring_z // 2 + ((i + 1) // 2) * (1 - 2 * ((i + 1) % 2))
        level = ((col // 2 + step) % ring_z) * 2
        for core in range(2):
            norm_copy(col, level + core).start()
        return carry

    lax.fori_loop(0, ring_z - 1, norm_send, 0)
    norm_copy(col, col + 1 - 2 * (col % 2)).start()
    pltpu.make_async_copy(
        sums_ref.at[pl.ds(0, n_dp - 1)], sums_ref.at[pl.ds(0, n_dp - 1)], semr_n
    ).wait()

    both = jnp.sum(sums_ref[...], axis=0)
    features = HEAD * HEADS_HERE * n_dp
    inv = lax.rsqrt(both[:CHUNKS] / features + 1e-06)
    bent = inv * inv * inv * both[CHUNKS:] / features
    norm_cols_ref[...] = jnp.concatenate(
        [inv, bent, jnp.zeros((CHUNK - 8, CHUNK), jnp.float32)], axis=0
    ).T

    scale = 1.0 / math.sqrt(ROWS * n_ctx)
    for h in range(HEADS_HERE):
        gain = gain_ref[:, part(h)]
        gain_part = jnp.zeros((1, HEAD), jnp.float32)
        for c in range(CHUNKS):
            raw = mix_ref[part(c), part(h)]
            grad = go_ref[part(c), part(h)].astype(jnp.float32)
            inv_c = norm_cols_ref[:, c : c + 1]
            bent_c = norm_cols_ref[:, CHUNKS + c : CHUNKS + c + 1]
            even = grad * inv_c
            gain_part += jnp.sum(even * raw, axis=0, keepdims=True)
            g_ref[part(c), part(h)] = (even * gain - raw * bent_c).astype(jnp.bfloat16)
        back = mxu(qw_ref[part(h), :], g_ref[:, part(h)], NN)
        send_b[h * per_head : (h + 1) * per_head, :piece, :] = back.reshape(
            per_head, piece, HEAD
        )
        send_b[h * per_head : (h + 1) * per_head, piece:, :] = jnp.broadcast_to(
            (gain_part * scale)[None], (per_head, EXTRA, HEAD)
        )
        spread_head(h, send_b, recv_b, sems_b, semr_b)

    for h in range(HEADS_HERE):
        for c in range(CHUNKS):
            attended_ref[part(c), part(h)] = (
                mix_ref[part(c), part(h)]
                * norm_cols_ref[:, c : c + 1]
                * gain_ref[:, part(h)]
            ).astype(jnp.bfloat16)

    def backward_part(h):
        start = start_ref[h * per_head : (h + 1) * per_head].reshape(HEAD, HEAD)
        start = start.astype(jnp.bfloat16)
        for i in range(CHUNKS):
            upto = slice(0, (i + 1) * CHUNK)
            rows = g_ref[part(i), part(h)]
            scores = mxu(rows, v_ref[upto, part(h)], NT)
            for j in range(i + 1):
                gw_ref[h, part(i), part(j)] = (
                    scores[:, part(j)] * gap_ref[h, part(i), part(j)]
                ).astype(jnp.bfloat16)
            local = mxu(gw_ref[h, part(i), upto], k_ref[upto, part(h)], NN)
            carried = mxu(rows, start, NT)
            gq_ref[part(i), part(h)] = (column(1, h, i) * carried + local).astype(
                jnp.bfloat16
            )
        for j in range(CHUNKS):
            down = slice(j * CHUNK, ROWS)
            lk_ref[part(j), part(h)] = mxu(
                gw_ref[h, down, part(j)], q_ref[down, part(h)], TN
            )
            lv_ref[part(j), part(h)] = mxu(
                weighted_ref[h, down, part(j)], g_ref[down, part(h)], TN
            )

    backward_part(0)
    backward_part(1)

    def scan_backward(i, carry):
        running, gain_sum = carry
        line = ring_y - 1 - i
        first = line * ring_x
        wait_group(first, ring_x, taken, send_b, recv_b, semr_b.at[line])
        for x in reversed(range(ring_x)):
            there = first + x
            give_back(there, running, back_b, end_ref, sems_bb, semr_bb)
            arrived = recv_b[pl.ds(there, 1)][0]
            decay = jnp.exp(recv_f[pl.ds(there, 1)][0, piece : piece + 1])
            running = decay * running + arrived[:piece]
            gain_sum = gain_sum + arrived[piece : piece + 1]
        return running, gain_sum

    nothing = jnp.zeros((1, HEAD), jnp.float32)
    _, gain_sum = lax.fori_loop(
        0, ring_y, scan_backward, (jnp.zeros((piece, HEAD), jnp.float32), nothing)
    )

    one_row = pl.ds(0, 1)

    @pl.when(me % per_head == 0)
    def _():
        gain_out[...] = jnp.broadcast_to(gain_sum, (8, HEAD))
        pltpu.make_async_copy(
            gain_out.at[one_row], gain_in.at[my_head, one_row], semr_g
        ).start()

        def tell(i, carry):
            pltpu.make_async_remote_copy(
                src_ref=gain_out.at[one_row],
                dst_ref=gain_in.at[my_head, one_row],
                send_sem=sems_g,
                recv_sem=semr_g,
                device_id={"ctx": (me + n_ctx // 2 + i) % n_ctx},
                device_id_type=MESH,
            ).start()
            return carry

        lax.fori_loop(0, n_ctx // 2, tell, 0)
        lax.fori_loop(n_ctx // 2 + 1, n_ctx, tell, 0)

    backward_part(2)
    backward_part(3)

    for h in range(HEADS_HERE):
        wait_group(
            h * per_head, per_head, given, back_b, end_ref, semr_bb.at[h]
        )
    pltpu.make_async_copy(
        gain_in.at[:, one_row], gain_in.at[:, one_row], semr_g
    ).wait()
    for h in range(HEADS_HERE):
        gg_ref[:, part(h)] = gain_in[h, 0:1]

    @pl.when(me % per_head == 0)
    def _():
        pltpu.make_async_copy(
            recv_f.at[pl.ds(0, n_ctx - 1), one_row],
            recv_b.at[pl.ds(0, n_ctx - 1), one_row],
            sems_g,
        ).wait()

    wait_group(0, n_ctx - 1, taken, send_f, recv_f, sems_f)
    wait_group(0, n_ctx - 1, given, back_f, start_ref, sems_fb)
    wait_group(0, n_ctx - 1, taken, send_b, recv_b, sems_b)
    wait_group(0, n_ctx - 1, given, back_b, end_ref, sems_bb)
    pltpu.make_async_copy(
        sums_ref.at[pl.ds(0, n_dp - 1)], sums_ref.at[pl.ds(0, n_dp - 1)], sems_n
    ).wait()


def finish(
    attended_ref,
    gq_ref,
    gg_ref,
    k_ref,
    v_ref,
    cols_ref,
    lk_ref,
    lv_ref,
    end_ref,
    attended_out,
    gq_out,
    gk_out,
    gv_out,
    gg_out,
    gk_ref,
    gv_ref,
    sems,
):
    copies = [
        pltpu.make_async_copy(source, target, sems.at[i])
        for i, (source, target) in enumerate(
            ((attended_ref, attended_out), (gq_ref, gq_out), (gg_ref, gg_out))
        )
    ]
    for copy in copies:
        copy.start()
    piece = end_ref.shape[1]
    per_head = HEAD // piece
    for c in range(CHUNKS):
        for h in range(HEADS_HERE):
            end = end_ref[h * per_head : (h + 1) * per_head].reshape(HEAD, HEAD)
            end = end.astype(jnp.bfloat16)
            at = 32 + c * HEADS_HERE + h
            fade = cols_ref[:, at : at + 1]
            gk_ref[part(c), part(h)] = (
                fade * mxu(v_ref[part(c), part(h)], end, NT)
                + lk_ref[part(c), part(h)]
            ).astype(jnp.bfloat16)
            gv_ref[part(c), part(h)] = (
                fade * mxu(k_ref[part(c), part(h)], end, NN)
                + lv_ref[part(c), part(h)]
            ).astype(jnp.bfloat16)
        for i, (source, target) in enumerate(((gk_ref, gk_out), (gv_ref, gv_out))):
            copy = pltpu.make_async_copy(
                source.at[part(c)], target.at[part(c)], sems.at[3 + 2 * c + i]
            )
            copy.start()
            copies.append(copy)
    for copy in copies:
        copy.wait()


def on_device(
    n_ctx, n_dp, ring_x, query_in, key_in, value_in, log_decay, norm_gain, grad_out
):
    width = HEAD * HEADS_HERE
    piece = ROWS // n_ctx
    full = jax.ShapeDtypeStruct((ROWS, width), jnp.bfloat16)
    f32, bf16 = jnp.float32, jnp.bfloat16
    message = pltpu.VMEM((n_ctx, piece + EXTRA, HEAD), f32)
    plain = pltpu.VMEM((n_ctx, piece, HEAD), f32)
    vmem = pl.BlockSpec(memory_space=pltpu.VMEM)
    hbm = pl.BlockSpec(memory_space=pltpu.HBM)
    outs = pl.pallas_call(
        functools.partial(kernel, n_ctx, n_dp, ring_x),
        out_shape=[
            full,
            full,
            jax.ShapeDtypeStruct((1, width), f32),
            full,
            full,
            jax.ShapeDtypeStruct((CHUNK, CHUNK), f32),
            jax.ShapeDtypeStruct((ROWS, width), f32),
            jax.ShapeDtypeStruct((ROWS, width), f32),
            jax.ShapeDtypeStruct((n_ctx, piece, HEAD), f32),
        ],
        in_specs=[hbm] * 6,
        out_specs=[vmem] * 9,
        scratch_shapes=[
            pltpu.VMEM((ROWS, width), bf16),
            pltpu.VMEM((HEADS_HERE, ROWS), f32),
            pltpu.VMEM((1, width), f32),
            pltpu.VMEM((ROWS, width), bf16),
            pltpu.SemaphoreType.DMA((6,)),
            pltpu.VMEM((16, CHUNK), f32),
            pltpu.VMEM((HEADS_HERE, ROWS, ROWS), f32),
            pltpu.VMEM((HEADS_HERE, ROWS, ROWS), bf16),
            pltpu.VMEM((HEADS_HERE, ROWS, ROWS), bf16),
            pltpu.VMEM((ROWS, width), f32),
            pltpu.VMEM((ROWS, width), bf16),
            pltpu.VMEM((width, ROWS), bf16),
            message,
            message,
            plain,
            plain,
            message,
            message,
            plain,
            pltpu.VMEM((8, HEAD), f32),
            pltpu.VMEM((HEADS_HERE, 8, HEAD), f32),
            pltpu.VMEM((n_dp, 8, CHUNK), f32),
            pltpu.VMEM((CHUNK, CHUNK), f32),
        ]
        + [
            pltpu.SemaphoreType.DMA,
            pltpu.SemaphoreType.DMA((n_ctx // ring_x,)),
            pltpu.SemaphoreType.DMA,
            pltpu.SemaphoreType.DMA((HEADS_HERE,)),
        ]
        * 2
        + [pltpu.SemaphoreType.DMA] * 4,
        compiler_params=pltpu.CompilerParams(
            collective_id=0,
            has_side_effects=True,
            vmem_limit_bytes=VMEM_BYTES,
        ),
        name="lightning",
    )(
        *(
            pltpu.with_memory_space_constraint(array, pltpu.HBM)
            for array in (
                query_in,
                key_in,
                value_in,
                log_decay,
                norm_gain.reshape(1, width),
                grad_out,
            )
        )
    )
    stored = pl.pallas_call(
        finish,
        out_shape=[full] * 4 + [jax.ShapeDtypeStruct((1, width), f32)],
        in_specs=[vmem] * 9,
        out_specs=[hbm] * 5,
        scratch_shapes=[
            pltpu.VMEM((ROWS, width), bf16),
            pltpu.VMEM((ROWS, width), bf16),
            pltpu.SemaphoreType.DMA((3 + 2 * CHUNKS,)),
        ],
        compiler_params=pltpu.CompilerParams(vmem_limit_bytes=4 * 1024 * 1024),
        name="finish",
    )(*outs)
    return (*stored[:4], stored[4].reshape(width))


def solution(mesh):
    in_specs = (
        P("ctx", "dp"),
        P("ctx", "dp"),
        P("ctx", "dp"),
        P("dp", "ctx"),
        P("dp"),
        P("ctx", "dp"),
    )
    out_specs = (P("ctx", "dp"), P("ctx", "dp"), P("ctx", "dp"), P("ctx", "dp"), P("dp"))
    n_ctx, n_dp = mesh.shape["ctx"], mesh.shape["dp"]
    return jax.shard_map(
        functools.partial(on_device, n_ctx, n_dp, min(RING_X, n_ctx // 2)),
        mesh=mesh,
        in_specs=in_specs,
        out_specs=out_specs,
        check_vma=False,
    )
```

```python
import functools
import math

import jax
import jax.numpy as jnp
from jax import lax
from jax.experimental import pallas as pl
from jax.experimental.pallas import tpu as pltpu
from jax.sharding import PartitionSpec as P

MESH = pl.DeviceIdType.MESH
HEAD = 128
HEADS_HERE = 4
CHUNK = 128
CHUNKS = 4
ROWS = CHUNK * CHUNKS
EXTRA = 8
RING_X = 4
VMEM_BYTES = 48 * 1024 * 1024

NT = (((1,), (1,)), ((), ()))
NN = (((1,), (0,)), ((), ()))
TN = (((0,), (0,)), ((), ()))


def mxu(left, right, form):
    return lax.dot_general(left, right, form, preferred_element_type=jnp.float32)


def split(terms):
    high = terms.astype(jnp.bfloat16)
    return high, (terms - high.astype(jnp.float32)).astype(jnp.bfloat16)


def part(index):
    return slice(index * CHUNK, (index + 1) * CHUNK)


def kernel(
    n_ctx,
    n_dp,
    ring_x,
    q_hbm,
    k_hbm,
    v_hbm,
    decay_hbm,
    gain_hbm,
    go_hbm,
    attended_ref,
    gq_ref,
    gg_ref,
    k_ref,
    v_ref,
    cols_ref,
    lk_ref,
    lv_ref,
    end_ref,
    q_ref,
    decay_ref,
    gain_ref,
    go_ref,
    sem_in,
    rows_ref,
    gap_ref,
    weighted_ref,
    gw_ref,
    mix_ref,
    g_ref,
    qw_ref,
    send_f,
    recv_f,
    back_f,
    start_ref,
    send_b,
    recv_b,
    back_b,
    gain_out,
    gain_in,
    sums_ref,
    norm_cols_ref,
    sems_f,
    semr_f,
    sems_fb,
    semr_fb,
    sems_b,
    semr_b,
    sems_bb,
    semr_bb,
    sems_n,
    semr_n,
    sems_g,
    semr_g,
):
    me = lax.axis_index("ctx")
    col = lax.axis_index("dp")
    piece = ROWS // n_ctx
    half = piece // 2
    per_head = HEAD // piece
    ring_y = n_ctx // ring_x
    my_y, my_x = me // ring_x, me % ring_x
    my_head = me // per_head
    ring_z = n_dp // 2
    far_x = sorted(range(ring_x), key=lambda d: -min(d, ring_x - d))

    loads = [
        pltpu.make_async_copy(source, target, sem_in.at[i])
        for i, (source, target) in enumerate(
            (
                (decay_hbm, decay_ref),
                (k_hbm, k_ref),
                (v_hbm, v_ref),
                (q_hbm, q_ref),
                (gain_hbm, gain_ref),
                (go_hbm, go_ref),
            )
        )
    ]
    for load in loads:
        load.start()
    barrier = pltpu.get_barrier_semaphore()

    def far_line(i):
        step = ring_y // 2 + ((i + 1) // 2) * (1 - 2 * ((i + 1) % 2))
        return ((my_y + step) % ring_y) * ring_x

    def greet(there):
        pl.semaphore_signal(
            barrier, inc=1, device_id={"ctx": there}, device_id_type=MESH
        )

    def greet_line(i, carry):
        line = far_line(i)
        for step_x in far_x:
            greet(line + (my_x + step_x) % ring_x)
        return carry

    lax.fori_loop(0, ring_y - 1, greet_line, 0)
    for step_x in far_x[:-1]:
        greet(my_y * ring_x + (my_x + step_x) % ring_x)

    def greet_dp(i, carry):
        pl.semaphore_signal(
            barrier, inc=1, device_id={"dp": (col + i) % n_dp}, device_id_type=MESH
        )
        return carry

    lax.fori_loop(1, n_dp, greet_dp, 0)

    loads[0].wait()
    logs = decay_ref[...]
    stacked = jnp.concatenate([logs[:, part(c)] for c in range(CHUNKS)], axis=0)
    high = stacked.astype(jnp.bfloat16)
    rest = stacked - high.astype(jnp.float32)
    middle = rest.astype(jnp.bfloat16)
    low = (rest - middle.astype(jnp.float32)).astype(jnp.bfloat16)
    row_i = lax.broadcasted_iota(jnp.int32, (CHUNK, 2 * CHUNK), 0)
    col_i = lax.broadcasted_iota(jnp.int32, (CHUNK, 2 * CHUNK), 1)
    adder = jnp.where(row_i <= col_i, 1.0, 0.0).astype(jnp.bfloat16)
    sums = mxu(jnp.concatenate([high, middle, low], axis=0), adder, NN)
    sums = sums[0:16] + sums[16:32] + sums[32:48]
    inside, chunk_total = sums[:, :CHUNK], sums[:, CHUNK:]
    before = jnp.zeros((HEADS_HERE, CHUNK), jnp.float32)
    within = []
    for c in range(CHUNKS):
        block = slice(c * HEADS_HERE, (c + 1) * HEADS_HERE)
        within.append(inside[block] + before)
        before = before + chunk_total[block]
    total = before
    within = jnp.concatenate(within, axis=0)
    tail = jnp.exp(jnp.concatenate([total] * CHUNKS, axis=0) - within)
    rows_ref[...] = within
    cols_ref[...] = jnp.concatenate(
        [within, jnp.exp(within), tail, jnp.zeros((CHUNK - 48, CHUNK), jnp.float32)],
        axis=0,
    ).T

    def column(kind, h, c):
        at = 16 * kind + c * HEADS_HERE + h
        return cols_ref[:, at : at + 1]

    loads[1].wait()
    loads[2].wait()

    def fill(target, h, state, extra):
        pieces = pl.ds(h * per_head, per_head)
        state = state.reshape(per_head, 2, half, HEAD)
        target[pieces, :half, :] = state[:, 0]
        target[pieces, half : half + EXTRA, :] = jnp.broadcast_to(
            extra[None], (per_head, EXTRA, HEAD)
        )
        target[pieces, half + EXTRA :, :] = state[:, 1]

    for h in range(HEADS_HERE):
        weighted_keys = jnp.concatenate(
            [
                (k_ref[part(c), part(h)].astype(jnp.float32) * column(2, h, c)).astype(
                    jnp.bfloat16
                )
                for c in range(CHUNKS)
            ],
            axis=0,
        )
        state = mxu(weighted_keys, v_ref[:, part(h)], TN)
        fill(send_f, h, state, total[h : h + 1])
    pl.semaphore_wait(barrier, n_ctx - 1 + n_dp - 1)

    taken, given = pl.ds(0, piece + 1), pl.ds(0, piece)
    taken_half = (pl.ds(0, half + 1), pl.ds(half + EXTRA, half))
    given_half = (pl.ds(0, half), pl.ds(half, half))

    def copy_to(there, rows, source, target, ss, rs):
        return pltpu.make_async_remote_copy(
            src_ref=source.at[there, rows],
            dst_ref=target.at[me, rows],
            send_sem=ss,
            recv_sem=rs,
            device_id={"ctx": there},
            device_id_type=MESH,
        )

    def own_copy(rows, source, target, rs):
        return pltpu.make_async_copy(source.at[me, rows], target.at[me, rows], rs)

    def wait_group(first, count, rows, source, target, rs):
        group = pl.ds(first, count)
        pltpu.make_async_copy(
            source.at[group, rows], target.at[group, rows], rs
        ).wait()

    def spread(which, source, target, ss, rs):
        rows, arrival = taken_half[which], rs.at[which * ring_y + my_y]
        own_copy(rows, source, target, arrival).start()

        def one(i, carry):
            line = far_line(i)
            for step_x in far_x:
                there = line + (my_x + step_x) % ring_x
                copy_to(there, rows, source, target, ss, arrival).start()
            return carry

        lax.fori_loop(0, ring_y - 1, one, 0)
        for step_x in far_x[:-1]:
            there = my_y * ring_x + (my_x + step_x) % ring_x
            copy_to(there, rows, source, target, ss, arrival).start()

    def spread_head(h, source, target, ss, rs):
        rows, arrival = taken_half[0], rs.at[my_y]

        def one(there, carry):
            @pl.when(there != me)
            def _():
                copy_to(there, rows, source, target, ss, arrival).start()

            @pl.when(there == me)
            def _():
                own_copy(rows, source, target, arrival).start()

            return carry

        lax.fori_loop(h * per_head, (h + 1) * per_head, one, 0)

    def give_back(which, there, running, source, target, ss, rs):
        rows = given_half[which]
        source[pl.ds(there, 1), rows] = running[None]

        @pl.when(there != me)
        def _():
            copy_to(there, rows, source, target, ss, rs.at[my_head]).start()

        @pl.when(there == me)
        def _():
            own_copy(rows, source, target, rs.at[my_head]).start()

    spread(0, send_f, recv_f, sems_f, semr_f)
    spread(1, send_f, recv_f, sems_f, semr_f)

    for load in loads[3:]:
        load.wait()

    diag_t = lax.broadcasted_iota(jnp.int32, (CHUNK, CHUNK), 0)
    diag_s = lax.broadcasted_iota(jnp.int32, (CHUNK, CHUNK), 1)

    def forward_part(h):
        for i in range(CHUNKS):
            scores = mxu(
                q_ref[part(i), part(h)], k_ref[: (i + 1) * CHUNK, part(h)], NT
            )
            here = column(0, h, i)
            for j in range(i + 1):
                at = j * HEADS_HERE + h
                gap = here - rows_ref[at : at + 1, :]
                if i == j:
                    gap = jnp.where(diag_t >= diag_s, gap, -1e30)
                weight = jnp.exp(gap)
                gap_ref[h, part(i), part(j)] = weight
                weighted_ref[h, part(i), part(j)] = (
                    scores[:, part(j)] * weight
                ).astype(jnp.bfloat16)
            mix_ref[part(i), part(h)] = mxu(
                weighted_ref[h, part(i), : (i + 1) * CHUNK],
                v_ref[: (i + 1) * CHUNK, part(h)],
                NN,
            )
            qw_ref[part(h), part(i)] = (
                (q_ref[part(i), part(h)].astype(jnp.float32) * column(1, h, i)).T
            ).astype(jnp.bfloat16)

    forward_part(0)

    def half_rows(source, there, which):
        return source[pl.ds(there, 1), pl.ds(which * (half + EXTRA), half)][0]

    def extra_row(source, there):
        return source[pl.ds(there, 1), pl.ds(half, 1)][0]

    def scan_forward(which, line, running):
        first = line * ring_x
        arrival = semr_f.at[which * ring_y + line]
        wait_group(first, ring_x, taken_half[which], send_f, recv_f, arrival)
        for x in range(ring_x):
            there = first + x
            give_back(which, there, running, back_f, start_ref, sems_fb, semr_fb)
            decay = jnp.exp(extra_row(recv_f, there))
            running = decay * running + half_rows(recv_f, there, which)
        return running

    zero = jnp.zeros((half, HEAD), jnp.float32)
    for which in range(2):
        lax.fori_loop(0, ring_y, functools.partial(scan_forward, which), zero)

    forward_part(1)
    forward_part(2)
    forward_part(3)

    for h in range(HEADS_HERE):
        wait_group(
            h * per_head, per_head, given, back_f, start_ref, semr_fb.at[h]
        )
        start = start_ref[h * per_head : (h + 1) * per_head].reshape(HEAD, HEAD)
        start = start.astype(jnp.bfloat16)
        for c in range(CHUNKS):
            carried = mxu(q_ref[part(c), part(h)], start, NN)
            mix_ref[part(c), part(h)] += column(1, h, c) * carried

    squares, crosses = [], []
    for c in range(CHUNKS):
        square = jnp.zeros((CHUNK, HEAD), jnp.float32)
        cross = jnp.zeros((CHUNK, HEAD), jnp.float32)
        for h in range(HEADS_HERE):
            raw = mix_ref[part(c), part(h)]
            square += raw * raw
            cross += (
                go_ref[part(c), part(h)].astype(jnp.float32) * gain_ref[:, part(h)]
            ) * raw
        squares.append(jnp.concatenate(split(square), axis=1))
        crosses.append(jnp.concatenate(split(cross), axis=1))
    ones = jnp.ones((16, 2 * HEAD), jnp.bfloat16)
    row_sums = mxu(ones, jnp.concatenate(squares + crosses, axis=0), NT)[0:1]
    sums_ref[pl.ds(col, 1)] = jnp.concatenate(
        [row_sums[:, part(c)] for c in range(2 * CHUNKS)], axis=0
    )[None]

    def norm_copy(slot, there):
        return pltpu.make_async_remote_copy(
            src_ref=sums_ref.at[slot],
            dst_ref=sums_ref.at[slot],
            send_sem=sems_n,
            recv_sem=semr_n,
            device_id={"dp": there},
            device_id_type=MESH,
        )

    def norm_send(i, carry):
        step = ring_z // 2 + ((i + 1) // 2) * (1 - 2 * ((i + 1) % 2))
        level = ((col // 2 + step) % ring_z) * 2
        for core in range(2):
            norm_copy(col, level + core).start()
        return carry

    lax.fori_loop(0, ring_z - 1, norm_send, 0)
    norm_copy(col, col + 1 - 2 * (col % 2)).start()
    pltpu.make_async_copy(
        sums_ref.at[pl.ds(0, n_dp - 1)], sums_ref.at[pl.ds(0, n_dp - 1)], semr_n
    ).wait()

    both = jnp.sum(sums_ref[...], axis=0)
    features = HEAD * HEADS_HERE * n_dp
    inv = lax.rsqrt(both[:CHUNKS] / features + 1e-06)
    bent = inv * inv * inv * both[CHUNKS:] / features
    norm_cols_ref[...] = jnp.concatenate(
        [inv, bent, jnp.zeros((CHUNK - 8, CHUNK), jnp.float32)], axis=0
    ).T

    scale = 1.0 / math.sqrt(ROWS * n_ctx)
    for h in range(HEADS_HERE):
        gain = gain_ref[:, part(h)]
        gain_part = jnp.zeros((1, HEAD), jnp.float32)
        for c in range(CHUNKS):
            raw = mix_ref[part(c), part(h)]
            grad = go_ref[part(c), part(h)].astype(jnp.float32)
            inv_c = norm_cols_ref[:, c : c + 1]
            bent_c = norm_cols_ref[:, CHUNKS + c : CHUNKS + c + 1]
            even = grad * inv_c
            gain_part += jnp.sum(even * raw, axis=0, keepdims=True)
            g_ref[part(c), part(h)] = (even * gain - raw * bent_c).astype(jnp.bfloat16)
        back = mxu(qw_ref[part(h), :], g_ref[:, part(h)], NN)
        fill(send_b, h, back, gain_part * scale)
        spread_head(h, send_b, recv_b, sems_b, semr_b)
    spread(1, send_b, recv_b, sems_b, semr_b)

    for h in range(HEADS_HERE):
        for c in range(CHUNKS):
            attended_ref[part(c), part(h)] = (
                mix_ref[part(c), part(h)]
                * norm_cols_ref[:, c : c + 1]
                * gain_ref[:, part(h)]
            ).astype(jnp.bfloat16)

    def backward_part(h):
        start = start_ref[h * per_head : (h + 1) * per_head].reshape(HEAD, HEAD)
        start = start.astype(jnp.bfloat16)
        for i in range(CHUNKS):
            upto = slice(0, (i + 1) * CHUNK)
            rows = g_ref[part(i), part(h)]
            scores = mxu(rows, v_ref[upto, part(h)], NT)
            for j in range(i + 1):
                gw_ref[h, part(i), part(j)] = (
                    scores[:, part(j)] * gap_ref[h, part(i), part(j)]
                ).astype(jnp.bfloat16)
            local = mxu(gw_ref[h, part(i), upto], k_ref[upto, part(h)], NN)
            carried = mxu(rows, start, NT)
            gq_ref[part(i), part(h)] = (column(1, h, i) * carried + local).astype(
                jnp.bfloat16
            )
        for j in range(CHUNKS):
            down = slice(j * CHUNK, ROWS)
            lk_ref[part(j), part(h)] = mxu(
                gw_ref[h, down, part(j)], q_ref[down, part(h)], TN
            )
            lv_ref[part(j), part(h)] = mxu(
                weighted_ref[h, down, part(j)], g_ref[down, part(h)], TN
            )

    backward_part(0)
    backward_part(1)

    def scan_backward(which, i, carry):
        running, gain_sum = carry
        line = ring_y - 1 - i
        first = line * ring_x
        arrival = semr_b.at[which * ring_y + line]
        wait_group(first, ring_x, taken_half[which], send_b, recv_b, arrival)
        for x in reversed(range(ring_x)):
            there = first + x
            give_back(which, there, running, back_b, end_ref, sems_bb, semr_bb)
            decay = jnp.exp(extra_row(recv_f, there))
            running = decay * running + half_rows(recv_b, there, which)
            gain_sum = gain_sum + extra_row(recv_b, there)
        return running, gain_sum

    sums = []
    for which in range(2):
        turn = functools.partial(scan_backward, which)
        nothing = jnp.zeros((1, HEAD), jnp.float32)
        sums.append(lax.fori_loop(0, ring_y, turn, (zero, nothing))[1])
    gain_sum = sums[0]

    one_row = pl.ds(0, 1)

    @pl.when(me % per_head == 0)
    def _():
        gain_out[...] = jnp.broadcast_to(gain_sum, (8, HEAD))
        pltpu.make_async_copy(
            gain_out.at[one_row], gain_in.at[my_head, one_row], semr_g
        ).start()

        def tell(i, carry):
            pltpu.make_async_remote_copy(
                src_ref=gain_out.at[one_row],
                dst_ref=gain_in.at[my_head, one_row],
                send_sem=sems_g,
                recv_sem=semr_g,
                device_id={"ctx": (me + n_ctx // 2 + i) % n_ctx},
                device_id_type=MESH,
            ).start()
            return carry

        lax.fori_loop(0, n_ctx // 2, tell, 0)
        lax.fori_loop(n_ctx // 2 + 1, n_ctx, tell, 0)

    backward_part(2)
    backward_part(3)

    for h in range(HEADS_HERE):
        wait_group(
            h * per_head, per_head, given, back_b, end_ref, semr_bb.at[h]
        )
    pltpu.make_async_copy(
        gain_in.at[:, one_row], gain_in.at[:, one_row], semr_g
    ).wait()
    for h in range(HEADS_HERE):
        gg_ref[:, part(h)] = gain_in[h, 0:1]

    @pl.when(me % per_head == 0)
    def _():
        pltpu.make_async_copy(
            recv_f.at[pl.ds(0, n_ctx - 1), one_row],
            recv_b.at[pl.ds(0, n_ctx - 1), one_row],
            sems_g,
        ).wait()

    wait_group(0, n_ctx - 1, taken, send_f, recv_f, sems_f)
    wait_group(0, n_ctx - 1, given, back_f, start_ref, sems_fb)
    wait_group(0, n_ctx - 1, taken, send_b, recv_b, sems_b)
    wait_group(0, n_ctx - 1, given, back_b, end_ref, sems_bb)
    pltpu.make_async_copy(
        sums_ref.at[pl.ds(0, n_dp - 1)], sums_ref.at[pl.ds(0, n_dp - 1)], sems_n
    ).wait()


def finish(
    attended_ref,
    gq_ref,
    gg_ref,
    k_ref,
    v_ref,
    cols_ref,
    lk_ref,
    lv_ref,
    end_ref,
    attended_out,
    gq_out,
    gk_out,
    gv_out,
    gg_out,
    gk_ref,
    gv_ref,
    sems,
):
    copies = [
        pltpu.make_async_copy(source, target, sems.at[i])
        for i, (source, target) in enumerate(
            ((attended_ref, attended_out), (gq_ref, gq_out), (gg_ref, gg_out))
        )
    ]
    for copy in copies:
        copy.start()
    piece = end_ref.shape[1]
    per_head = HEAD // piece
    for c in range(CHUNKS):
        for h in range(HEADS_HERE):
            end = end_ref[h * per_head : (h + 1) * per_head].reshape(HEAD, HEAD)
            end = end.astype(jnp.bfloat16)
            at = 32 + c * HEADS_HERE + h
            fade = cols_ref[:, at : at + 1]
            gk_ref[part(c), part(h)] = (
                fade * mxu(v_ref[part(c), part(h)], end, NT)
                + lk_ref[part(c), part(h)]
            ).astype(jnp.bfloat16)
            gv_ref[part(c), part(h)] = (
                fade * mxu(k_ref[part(c), part(h)], end, NN)
                + lv_ref[part(c), part(h)]
            ).astype(jnp.bfloat16)
        for i, (source, target) in enumerate(((gk_ref, gk_out), (gv_ref, gv_out))):
            copy = pltpu.make_async_copy(
                source.at[part(c)], target.at[part(c)], sems.at[3 + 2 * c + i]
            )
            copy.start()
            copies.append(copy)
    for copy in copies:
        copy.wait()


def on_device(
    n_ctx, n_dp, ring_x, query_in, key_in, value_in, log_decay, norm_gain, grad_out
):
    width = HEAD * HEADS_HERE
    piece = ROWS // n_ctx
    full = jax.ShapeDtypeStruct((ROWS, width), jnp.bfloat16)
    f32, bf16 = jnp.float32, jnp.bfloat16
    message = pltpu.VMEM((n_ctx, piece + EXTRA, HEAD), f32)
    plain = pltpu.VMEM((n_ctx, piece, HEAD), f32)
    vmem = pl.BlockSpec(memory_space=pltpu.VMEM)
    hbm = pl.BlockSpec(memory_space=pltpu.HBM)
    outs = pl.pallas_call(
        functools.partial(kernel, n_ctx, n_dp, ring_x),
        out_shape=[
            full,
            full,
            jax.ShapeDtypeStruct((1, width), f32),
            full,
            full,
            jax.ShapeDtypeStruct((CHUNK, CHUNK), f32),
            jax.ShapeDtypeStruct((ROWS, width), f32),
            jax.ShapeDtypeStruct((ROWS, width), f32),
            jax.ShapeDtypeStruct((n_ctx, piece, HEAD), f32),
        ],
        in_specs=[hbm] * 6,
        out_specs=[vmem] * 9,
        scratch_shapes=[
            pltpu.VMEM((ROWS, width), bf16),
            pltpu.VMEM((HEADS_HERE, ROWS), f32),
            pltpu.VMEM((1, width), f32),
            pltpu.VMEM((ROWS, width), bf16),
            pltpu.SemaphoreType.DMA((6,)),
            pltpu.VMEM((16, CHUNK), f32),
            pltpu.VMEM((HEADS_HERE, ROWS, ROWS), f32),
            pltpu.VMEM((HEADS_HERE, ROWS, ROWS), bf16),
            pltpu.VMEM((HEADS_HERE, ROWS, ROWS), bf16),
            pltpu.VMEM((ROWS, width), f32),
            pltpu.VMEM((ROWS, width), bf16),
            pltpu.VMEM((width, ROWS), bf16),
            message,
            message,
            plain,
            plain,
            message,
            message,
            plain,
            pltpu.VMEM((8, HEAD), f32),
            pltpu.VMEM((HEADS_HERE, 8, HEAD), f32),
            pltpu.VMEM((n_dp, 8, CHUNK), f32),
            pltpu.VMEM((CHUNK, CHUNK), f32),
        ]
        + [
            pltpu.SemaphoreType.DMA,
            pltpu.SemaphoreType.DMA((2 * n_ctx // ring_x,)),
            pltpu.SemaphoreType.DMA,
            pltpu.SemaphoreType.DMA((HEADS_HERE,)),
        ]
        * 2
        + [pltpu.SemaphoreType.DMA] * 4,
        compiler_params=pltpu.CompilerParams(
            collective_id=0,
            has_side_effects=True,
            vmem_limit_bytes=VMEM_BYTES,
        ),
        name="lightning",
    )(
        *(
            pltpu.with_memory_space_constraint(array, pltpu.HBM)
            for array in (
                query_in,
                key_in,
                value_in,
                log_decay,
                norm_gain.reshape(1, width),
                grad_out,
            )
        )
    )
    stored = pl.pallas_call(
        finish,
        out_shape=[full] * 4 + [jax.ShapeDtypeStruct((1, width), f32)],
        in_specs=[vmem] * 9,
        out_specs=[hbm] * 5,
        scratch_shapes=[
            pltpu.VMEM((ROWS, width), bf16),
            pltpu.VMEM((ROWS, width), bf16),
            pltpu.SemaphoreType.DMA((3 + 2 * CHUNKS,)),
        ],
        compiler_params=pltpu.CompilerParams(vmem_limit_bytes=4 * 1024 * 1024),
        name="finish",
    )(*outs)
    return (*stored[:4], stored[4].reshape(width))


def solution(mesh):
    in_specs = (
        P("ctx", "dp"),
        P("ctx", "dp"),
        P("ctx", "dp"),
        P("dp", "ctx"),
        P("dp"),
        P("ctx", "dp"),
    )
    out_specs = (P("ctx", "dp"), P("ctx", "dp"), P("ctx", "dp"), P("ctx", "dp"), P("dp"))
    n_ctx, n_dp = mesh.shape["ctx"], mesh.shape["dp"]
    return jax.shard_map(
        functools.partial(on_device, n_ctx, n_dp, min(RING_X, n_ctx // 2)),
        mesh=mesh,
        in_specs=in_specs,
        out_specs=out_specs,
        check_vma=False,
    )
```

```python
import functools
import math

import jax
import jax.numpy as jnp
from jax import lax
from jax.experimental import pallas as pl
from jax.experimental.pallas import tpu as pltpu
from jax.sharding import PartitionSpec as P

MESH = pl.DeviceIdType.MESH
HEAD = 128
HEADS_HERE = 4
CHUNK = 128
CHUNKS = 4
ROWS = CHUNK * CHUNKS
EXTRA = 8
RING_X = 4
VMEM_BYTES = 48 * 1024 * 1024

NT = (((1,), (1,)), ((), ()))
NN = (((1,), (0,)), ((), ()))
TN = (((0,), (0,)), ((), ()))


def mxu(left, right, form):
    return lax.dot_general(left, right, form, preferred_element_type=jnp.float32)


def split(terms):
    high = terms.astype(jnp.bfloat16)
    return high, (terms - high.astype(jnp.float32)).astype(jnp.bfloat16)


def part(index):
    return slice(index * CHUNK, (index + 1) * CHUNK)


def kernel(
    n_ctx,
    n_dp,
    ring_x,
    q_hbm,
    k_hbm,
    v_hbm,
    decay_hbm,
    gain_hbm,
    go_hbm,
    attended_ref,
    gq_ref,
    gg_ref,
    k_ref,
    v_ref,
    cols_ref,
    lk_ref,
    lv_ref,
    end_ref,
    q_ref,
    decay_ref,
    gain_ref,
    go_ref,
    sem_in,
    rows_ref,
    gap_ref,
    weighted_ref,
    gw_ref,
    mix_ref,
    g_ref,
    qw_ref,
    send_f,
    recv_f,
    back_f,
    start_ref,
    send_b,
    recv_b,
    back_b,
    gain_out,
    gain_in,
    sums_ref,
    norm_cols_ref,
    sems_f,
    semr_f,
    sems_fb,
    semr_fb,
    sems_b,
    semr_b,
    sems_bb,
    semr_bb,
    sems_n,
    semr_n,
    sems_g,
    semr_g,
):
    me = lax.axis_index("ctx")
    col = lax.axis_index("dp")
    piece = ROWS // n_ctx
    half = piece // 2
    per_head = HEAD // piece
    ring_y = n_ctx // ring_x
    my_y, my_x = me // ring_x, me % ring_x
    my_head = me // per_head
    ring_z = n_dp // 2
    far_x = sorted(range(ring_x), key=lambda d: -min(d, ring_x - d))

    loads = [
        pltpu.make_async_copy(source, target, sem_in.at[i])
        for i, (source, target) in enumerate(
            (
                (decay_hbm, decay_ref),
                (k_hbm, k_ref),
                (v_hbm, v_ref),
                (q_hbm, q_ref),
                (gain_hbm, gain_ref),
                (go_hbm, go_ref),
            )
        )
    ]
    for load in loads:
        load.start()
    barrier = pltpu.get_barrier_semaphore()

    def far_line(i):
        step = ring_y // 2 + ((i + 1) // 2) * (1 - 2 * ((i + 1) % 2))
        return ((my_y + step) % ring_y) * ring_x

    def greet(there):
        pl.semaphore_signal(
            barrier, inc=1, device_id={"ctx": there}, device_id_type=MESH
        )

    def greet_line(i, carry):
        line = far_line(i)
        for step_x in far_x:
            greet(line + (my_x + step_x) % ring_x)
        return carry

    lax.fori_loop(0, ring_y - 1, greet_line, 0)
    for step_x in far_x[:-1]:
        greet(my_y * ring_x + (my_x + step_x) % ring_x)

    def greet_dp(i, carry):
        pl.semaphore_signal(
            barrier, inc=1, device_id={"dp": (col + i) % n_dp}, device_id_type=MESH
        )
        return carry

    lax.fori_loop(1, n_dp, greet_dp, 0)

    loads[0].wait()
    logs = decay_ref[...]
    stacked = jnp.concatenate([logs[:, part(c)] for c in range(CHUNKS)], axis=0)
    high = stacked.astype(jnp.bfloat16)
    rest = stacked - high.astype(jnp.float32)
    middle = rest.astype(jnp.bfloat16)
    low = (rest - middle.astype(jnp.float32)).astype(jnp.bfloat16)
    row_i = lax.broadcasted_iota(jnp.int32, (CHUNK, 2 * CHUNK), 0)
    col_i = lax.broadcasted_iota(jnp.int32, (CHUNK, 2 * CHUNK), 1)
    adder = jnp.where(row_i <= col_i, 1.0, 0.0).astype(jnp.bfloat16)
    sums = mxu(jnp.concatenate([high, middle, low], axis=0), adder, NN)
    sums = sums[0:16] + sums[16:32] + sums[32:48]
    inside, chunk_total = sums[:, :CHUNK], sums[:, CHUNK:]
    before = jnp.zeros((HEADS_HERE, CHUNK), jnp.float32)
    within = []
    for c in range(CHUNKS):
        block = slice(c * HEADS_HERE, (c + 1) * HEADS_HERE)
        within.append(inside[block] + before)
        before = before + chunk_total[block]
    total = before
    within = jnp.concatenate(within, axis=0)
    tail = jnp.exp(jnp.concatenate([total] * CHUNKS, axis=0) - within)
    rows_ref[...] = within
    cols_ref[...] = jnp.concatenate(
        [within, jnp.exp(within), tail, jnp.zeros((CHUNK - 48, CHUNK), jnp.float32)],
        axis=0,
    ).T

    def column(kind, h, c):
        at = 16 * kind + c * HEADS_HERE + h
        return cols_ref[:, at : at + 1]

    loads[1].wait()
    loads[2].wait()

    def fill(target, h, state, extra):
        pieces = pl.ds(h * per_head, per_head)
        state = state.reshape(per_head, 2, half, HEAD)
        target[pieces, :half, :] = state[:, 0]
        target[pieces, half : half + EXTRA, :] = jnp.broadcast_to(
            extra[None], (per_head, EXTRA, HEAD)
        )
        target[pieces, half + EXTRA :, :] = state[:, 1]

    for h in range(HEADS_HERE):
        weighted_keys = jnp.concatenate(
            [
                (k_ref[part(c), part(h)].astype(jnp.float32) * column(2, h, c)).astype(
                    jnp.bfloat16
                )
                for c in range(CHUNKS)
            ],
            axis=0,
        )
        state = mxu(weighted_keys, v_ref[:, part(h)], TN)
        fill(send_f, h, state, total[h : h + 1])
    pl.semaphore_wait(barrier, n_ctx - 1 + n_dp - 1)

    taken, given = pl.ds(0, piece + 1), pl.ds(0, piece)
    taken_half = (pl.ds(0, half + 1), pl.ds(half + EXTRA, half))
    given_half = (pl.ds(0, half), pl.ds(half, half))

    def copy_to(there, rows, source, target, ss, rs):
        return pltpu.make_async_remote_copy(
            src_ref=source.at[there, rows],
            dst_ref=target.at[me, rows],
            send_sem=ss,
            recv_sem=rs,
            device_id={"ctx": there},
            device_id_type=MESH,
        )

    def own_copy(rows, source, target, rs):
        return pltpu.make_async_copy(source.at[me, rows], target.at[me, rows], rs)

    def wait_group(first, count, rows, source, target, rs):
        group = pl.ds(first, count)
        pltpu.make_async_copy(
            source.at[group, rows], target.at[group, rows], rs
        ).wait()

    def spread(which, source, target, ss, rs):
        rows, arrival = taken_half[which], rs.at[which * ring_y + my_y]
        own_copy(rows, source, target, arrival).start()

        def one(i, carry):
            line = far_line(i)
            for step_x in far_x:
                there = line + (my_x + step_x) % ring_x
                copy_to(there, rows, source, target, ss, arrival).start()
            return carry

        lax.fori_loop(0, ring_y - 1, one, 0)
        for step_x in far_x[:-1]:
            there = my_y * ring_x + (my_x + step_x) % ring_x
            copy_to(there, rows, source, target, ss, arrival).start()

    def spread_head(h, source, target, ss, rs):
        rows, arrival = taken_half[0], rs.at[my_y]

        def one(there, carry):
            @pl.when(there != me)
            def _():
                copy_to(there, rows, source, target, ss, arrival).start()

            @pl.when(there == me)
            def _():
                own_copy(rows, source, target, arrival).start()

            return carry

        lax.fori_loop(h * per_head, (h + 1) * per_head, one, 0)

    def give_back(which, there, running, source, target, ss, rs):
        rows = given_half[which]
        source[pl.ds(there, 1), rows] = running[None]

        @pl.when(there != me)
        def _():
            copy_to(there, rows, source, target, ss, rs.at[my_head]).start()

        @pl.when(there == me)
        def _():
            own_copy(rows, source, target, rs.at[my_head]).start()

    spread(0, send_f, recv_f, sems_f, semr_f)
    spread(1, send_f, recv_f, sems_f, semr_f)

    for load in loads[3:]:
        load.wait()

    diag_t = lax.broadcasted_iota(jnp.int32, (CHUNK, CHUNK), 0)
    diag_s = lax.broadcasted_iota(jnp.int32, (CHUNK, CHUNK), 1)

    def forward_part(h):
        for i in range(CHUNKS):
            scores = mxu(
                q_ref[part(i), part(h)], k_ref[: (i + 1) * CHUNK, part(h)], NT
            )
            here = column(0, h, i)
            for j in range(i + 1):
                at = j * HEADS_HERE + h
                gap = here - rows_ref[at : at + 1, :]
                if i == j:
                    gap = jnp.where(diag_t >= diag_s, gap, -1e30)
                weight = jnp.exp(gap)
                gap_ref[h, part(i), part(j)] = weight
                weighted_ref[h, part(i), part(j)] = (
                    scores[:, part(j)] * weight
                ).astype(jnp.bfloat16)
            mix_ref[part(i), part(h)] = mxu(
                weighted_ref[h, part(i), : (i + 1) * CHUNK],
                v_ref[: (i + 1) * CHUNK, part(h)],
                NN,
            )
            qw_ref[part(h), part(i)] = (
                (q_ref[part(i), part(h)].astype(jnp.float32) * column(1, h, i)).T
            ).astype(jnp.bfloat16)

    forward_part(0)

    def half_rows(source, there, which):
        return source[pl.ds(there, 1), pl.ds(which * (half + EXTRA), half)][0]

    def extra_row(source, there):
        return source[pl.ds(there, 1), pl.ds(half, 1)][0]

    def scan_forward(which, line, running):
        first = line * ring_x
        arrival = semr_f.at[which * ring_y + line]
        wait_group(first, ring_x, taken_half[which], send_f, recv_f, arrival)
        for x in range(ring_x):
            there = first + x
            give_back(which, there, running, back_f, start_ref, sems_fb, semr_fb)
            decay = jnp.exp(extra_row(recv_f, there))
            running = decay * running + half_rows(recv_f, there, which)
        return running

    zero = jnp.zeros((half, HEAD), jnp.float32)
    for which in range(2):
        lax.fori_loop(0, ring_y, functools.partial(scan_forward, which), zero)

    forward_part(1)
    forward_part(2)
    forward_part(3)

    for h in range(HEADS_HERE):
        wait_group(
            h * per_head, per_head, given, back_f, start_ref, semr_fb.at[h]
        )
        start = start_ref[h * per_head : (h + 1) * per_head].reshape(HEAD, HEAD)
        start = start.astype(jnp.bfloat16)
        for c in range(CHUNKS):
            carried = mxu(q_ref[part(c), part(h)], start, NN)
            mix_ref[part(c), part(h)] += column(1, h, c) * carried

    squares, crosses = [], []
    for c in range(CHUNKS):
        square = jnp.zeros((CHUNK, HEAD), jnp.float32)
        cross = jnp.zeros((CHUNK, HEAD), jnp.float32)
        for h in range(HEADS_HERE):
            raw = mix_ref[part(c), part(h)]
            square += raw * raw
            cross += (
                go_ref[part(c), part(h)].astype(jnp.float32) * gain_ref[:, part(h)]
            ) * raw
        squares.append(jnp.concatenate(split(square), axis=1))
        crosses.append(jnp.concatenate(split(cross), axis=1))
    ones = jnp.ones((16, 2 * HEAD), jnp.bfloat16)
    row_sums = mxu(ones, jnp.concatenate(squares + crosses, axis=0), NT)[0:1]
    sums_ref[pl.ds(col, 1)] = jnp.concatenate(
        [row_sums[:, part(c)] for c in range(2 * CHUNKS)], axis=0
    )[None]

    def norm_copy(slot, there):
        return pltpu.make_async_remote_copy(
            src_ref=sums_ref.at[slot],
            dst_ref=sums_ref.at[slot],
            send_sem=sems_n,
            recv_sem=semr_n,
            device_id={"dp": there},
            device_id_type=MESH,
        )

    def norm_send(i, carry):
        step = ring_z // 2 + ((i + 1) // 2) * (1 - 2 * ((i + 1) % 2))
        level = ((col // 2 + step) % ring_z) * 2
        for core in range(2):
            norm_copy(col, level + core).start()
        return carry

    lax.fori_loop(0, ring_z - 1, norm_send, 0)
    norm_copy(col, col + 1 - 2 * (col % 2)).start()
    pltpu.make_async_copy(
        sums_ref.at[pl.ds(0, n_dp - 1)], sums_ref.at[pl.ds(0, n_dp - 1)], semr_n
    ).wait()

    both = jnp.sum(sums_ref[...], axis=0)
    features = HEAD * HEADS_HERE * n_dp
    inv = lax.rsqrt(both[:CHUNKS] / features + 1e-06)
    bent = inv * inv * inv * both[CHUNKS:] / features
    norm_cols_ref[...] = jnp.concatenate(
        [inv, bent, jnp.zeros((CHUNK - 8, CHUNK), jnp.float32)], axis=0
    ).T

    scale = 1.0 / math.sqrt(ROWS * n_ctx)
    for h in range(HEADS_HERE):
        gain = gain_ref[:, part(h)]
        gain_part = jnp.zeros((1, HEAD), jnp.float32)
        for c in range(CHUNKS):
            raw = mix_ref[part(c), part(h)]
            grad = go_ref[part(c), part(h)].astype(jnp.float32)
            inv_c = norm_cols_ref[:, c : c + 1]
            bent_c = norm_cols_ref[:, CHUNKS + c : CHUNKS + c + 1]
            even = grad * inv_c
            gain_part += jnp.sum(even * raw, axis=0, keepdims=True)
            g_ref[part(c), part(h)] = (even * gain - raw * bent_c).astype(jnp.bfloat16)
        back = mxu(qw_ref[part(h), :], g_ref[:, part(h)], NN)
        fill(send_b, h, back, gain_part * scale)
        spread_head(h, send_b, recv_b, sems_b, semr_b)
    spread(1, send_b, recv_b, sems_b, semr_b)

    for h in range(HEADS_HERE):
        for c in range(CHUNKS):
            attended_ref[part(c), part(h)] = (
                mix_ref[part(c), part(h)]
                * norm_cols_ref[:, c : c + 1]
                * gain_ref[:, part(h)]
            ).astype(jnp.bfloat16)

    def backward_part(h):
        start = start_ref[h * per_head : (h + 1) * per_head].reshape(HEAD, HEAD)
        start = start.astype(jnp.bfloat16)
        for i in range(CHUNKS):
            upto = slice(0, (i + 1) * CHUNK)
            rows = g_ref[part(i), part(h)]
            scores = mxu(rows, v_ref[upto, part(h)], NT)
            for j in range(i + 1):
                gw_ref[h, part(i), part(j)] = (
                    scores[:, part(j)] * gap_ref[h, part(i), part(j)]
                ).astype(jnp.bfloat16)
            local = mxu(gw_ref[h, part(i), upto], k_ref[upto, part(h)], NN)
            carried = mxu(rows, start, NT)
            gq_ref[part(i), part(h)] = (column(1, h, i) * carried + local).astype(
                jnp.bfloat16
            )
        for j in range(CHUNKS):
            down = slice(j * CHUNK, ROWS)
            lk_ref[part(j), part(h)] = mxu(
                gw_ref[h, down, part(j)], q_ref[down, part(h)], TN
            )
            lv_ref[part(j), part(h)] = mxu(
                weighted_ref[h, down, part(j)], g_ref[down, part(h)], TN
            )

    backward_part(0)
    backward_part(1)

    def scan_backward(which, i, carry):
        running, gain_sum = carry
        line = ring_y - 1 - i
        first = line * ring_x
        arrival = semr_b.at[which * ring_y + line]
        wait_group(first, ring_x, taken_half[which], send_b, recv_b, arrival)
        for x in reversed(range(ring_x)):
            there = first + x
            give_back(which, there, running, back_b, end_ref, sems_bb, semr_bb)
            decay = jnp.exp(extra_row(recv_f, there))
            running = decay * running + half_rows(recv_b, there, which)
            gain_sum = gain_sum + extra_row(recv_b, there)
        return running, gain_sum

    one_row = pl.ds(0, 1)
    told = n_ctx // per_head
    tells_itself = me // told == me % per_head

    def tell(i, carry):
        there = (me % per_head) * told + i
        source, target = gain_out.at[one_row], gain_in.at[my_head, one_row]

        @pl.when(there != me)
        def _():
            pltpu.make_async_remote_copy(
                src_ref=source,
                dst_ref=target,
                send_sem=sems_g,
                recv_sem=semr_g,
                device_id={"ctx": there},
                device_id_type=MESH,
            ).start()

        @pl.when(there == me)
        def _():
            pltpu.make_async_copy(source, target, semr_g).start()

        return carry

    def wait_told(count):
        rows = pl.ds(0, count)
        pltpu.make_async_copy(
            recv_f.at[rows, one_row], recv_b.at[rows, one_row], sems_g
        ).wait()

    nothing = jnp.zeros((1, HEAD), jnp.float32)
    turn = functools.partial(scan_backward, 0)
    _, gain_sum = lax.fori_loop(0, ring_y, turn, (zero, nothing))
    gain_out[...] = jnp.broadcast_to(gain_sum, (8, HEAD))
    lax.fori_loop(0, told, tell, 0)
    turn = functools.partial(scan_backward, 1)
    lax.fori_loop(0, ring_y, turn, (zero, nothing))

    backward_part(2)
    backward_part(3)

    for h in range(HEADS_HERE):
        wait_group(
            h * per_head, per_head, given, back_b, end_ref, semr_bb.at[h]
        )
    pltpu.make_async_copy(
        gain_in.at[:, one_row], gain_in.at[:, one_row], semr_g
    ).wait()
    for h in range(HEADS_HERE):
        gg_ref[:, part(h)] = gain_in[h, 0:1]

    @pl.when(tells_itself)
    def _():
        wait_told(told - 1)

    @pl.when(jnp.logical_not(tells_itself))
    def _():
        wait_told(told)

    wait_group(0, n_ctx - 1, taken, send_f, recv_f, sems_f)
    wait_group(0, n_ctx - 1, given, back_f, start_ref, sems_fb)
    wait_group(0, n_ctx - 1, taken, send_b, recv_b, sems_b)
    wait_group(0, n_ctx - 1, given, back_b, end_ref, sems_bb)
    pltpu.make_async_copy(
        sums_ref.at[pl.ds(0, n_dp - 1)], sums_ref.at[pl.ds(0, n_dp - 1)], sems_n
    ).wait()


def finish(
    attended_ref,
    gq_ref,
    gg_ref,
    k_ref,
    v_ref,
    cols_ref,
    lk_ref,
    lv_ref,
    end_ref,
    attended_out,
    gq_out,
    gk_out,
    gv_out,
    gg_out,
    gk_ref,
    gv_ref,
    sems,
):
    copies = [
        pltpu.make_async_copy(source, target, sems.at[i])
        for i, (source, target) in enumerate(
            ((attended_ref, attended_out), (gq_ref, gq_out), (gg_ref, gg_out))
        )
    ]
    for copy in copies:
        copy.start()
    piece = end_ref.shape[1]
    per_head = HEAD // piece
    for c in range(CHUNKS):
        for h in range(HEADS_HERE):
            end = end_ref[h * per_head : (h + 1) * per_head].reshape(HEAD, HEAD)
            end = end.astype(jnp.bfloat16)
            at = 32 + c * HEADS_HERE + h
            fade = cols_ref[:, at : at + 1]
            gk_ref[part(c), part(h)] = (
                fade * mxu(v_ref[part(c), part(h)], end, NT)
                + lk_ref[part(c), part(h)]
            ).astype(jnp.bfloat16)
            gv_ref[part(c), part(h)] = (
                fade * mxu(k_ref[part(c), part(h)], end, NN)
                + lv_ref[part(c), part(h)]
            ).astype(jnp.bfloat16)
        for i, (source, target) in enumerate(((gk_ref, gk_out), (gv_ref, gv_out))):
            copy = pltpu.make_async_copy(
                source.at[part(c)], target.at[part(c)], sems.at[3 + 2 * c + i]
            )
            copy.start()
            copies.append(copy)
    for copy in copies:
        copy.wait()


def on_device(
    n_ctx, n_dp, ring_x, query_in, key_in, value_in, log_decay, norm_gain, grad_out
):
    width = HEAD * HEADS_HERE
    piece = ROWS // n_ctx
    full = jax.ShapeDtypeStruct((ROWS, width), jnp.bfloat16)
    f32, bf16 = jnp.float32, jnp.bfloat16
    message = pltpu.VMEM((n_ctx, piece + EXTRA, HEAD), f32)
    plain = pltpu.VMEM((n_ctx, piece, HEAD), f32)
    vmem = pl.BlockSpec(memory_space=pltpu.VMEM)
    hbm = pl.BlockSpec(memory_space=pltpu.HBM)
    outs = pl.pallas_call(
        functools.partial(kernel, n_ctx, n_dp, ring_x),
        out_shape=[
            full,
            full,
            jax.ShapeDtypeStruct((1, width), f32),
            full,
            full,
            jax.ShapeDtypeStruct((CHUNK, CHUNK), f32),
            jax.ShapeDtypeStruct((ROWS, width), f32),
            jax.ShapeDtypeStruct((ROWS, width), f32),
            jax.ShapeDtypeStruct((n_ctx, piece, HEAD), f32),
        ],
        in_specs=[hbm] * 6,
        out_specs=[vmem] * 9,
        scratch_shapes=[
            pltpu.VMEM((ROWS, width), bf16),
            pltpu.VMEM((HEADS_HERE, ROWS), f32),
            pltpu.VMEM((1, width), f32),
            pltpu.VMEM((ROWS, width), bf16),
            pltpu.SemaphoreType.DMA((6,)),
            pltpu.VMEM((16, CHUNK), f32),
            pltpu.VMEM((HEADS_HERE, ROWS, ROWS), f32),
            pltpu.VMEM((HEADS_HERE, ROWS, ROWS), bf16),
            pltpu.VMEM((HEADS_HERE, ROWS, ROWS), bf16),
            pltpu.VMEM((ROWS, width), f32),
            pltpu.VMEM((ROWS, width), bf16),
            pltpu.VMEM((width, ROWS), bf16),
            message,
            message,
            plain,
            plain,
            message,
            message,
            plain,
            pltpu.VMEM((8, HEAD), f32),
            pltpu.VMEM((HEADS_HERE, 8, HEAD), f32),
            pltpu.VMEM((n_dp, 8, CHUNK), f32),
            pltpu.VMEM((CHUNK, CHUNK), f32),
        ]
        + [
            pltpu.SemaphoreType.DMA,
            pltpu.SemaphoreType.DMA((2 * n_ctx // ring_x,)),
            pltpu.SemaphoreType.DMA,
            pltpu.SemaphoreType.DMA((HEADS_HERE,)),
        ]
        * 2
        + [pltpu.SemaphoreType.DMA] * 4,
        compiler_params=pltpu.CompilerParams(
            collective_id=0,
            has_side_effects=True,
            vmem_limit_bytes=VMEM_BYTES,
        ),
        name="lightning",
    )(
        *(
            pltpu.with_memory_space_constraint(array, pltpu.HBM)
            for array in (
                query_in,
                key_in,
                value_in,
                log_decay,
                norm_gain.reshape(1, width),
                grad_out,
            )
        )
    )
    stored = pl.pallas_call(
        finish,
        out_shape=[full] * 4 + [jax.ShapeDtypeStruct((1, width), f32)],
        in_specs=[vmem] * 9,
        out_specs=[hbm] * 5,
        scratch_shapes=[
            pltpu.VMEM((ROWS, width), bf16),
            pltpu.VMEM((ROWS, width), bf16),
            pltpu.SemaphoreType.DMA((3 + 2 * CHUNKS,)),
        ],
        compiler_params=pltpu.CompilerParams(vmem_limit_bytes=4 * 1024 * 1024),
        name="finish",
    )(*outs)
    return (*stored[:4], stored[4].reshape(width))


def solution(mesh):
    in_specs = (
        P("ctx", "dp"),
        P("ctx", "dp"),
        P("ctx", "dp"),
        P("dp", "ctx"),
        P("dp"),
        P("ctx", "dp"),
    )
    out_specs = (P("ctx", "dp"), P("ctx", "dp"), P("ctx", "dp"), P("ctx", "dp"), P("dp"))
    n_ctx, n_dp = mesh.shape["ctx"], mesh.shape["dp"]
    return jax.shard_map(
        functools.partial(on_device, n_ctx, n_dp, min(RING_X, n_ctx // 2)),
        mesh=mesh,
        in_specs=in_specs,
        out_specs=out_specs,
        check_vma=False,
    )
```
